32 devices in a mesh: dp: 8 (over z, x), expert: 4 (over y, core).
Axes of the slice: x: 2, y: 2, z: 4, core: 2. Of those that a mesh axis runs over, the one named last changes fastest.
Arguments:
- out_grad: bfloat16 [4096, 4096], P(('dp', 'expert')), may hold values from -6 to 6
- expert_ids: int32 [4096, 4], P(('dp', 'expert')), may hold values from 0 to 15, all different within a row; in each aligned block of 128 rows (0 to 127, 128 to 255, ...) at most 48 rows name the same one
- gate_weights: bfloat16 [4096, 4], P(('dp', 'expert')), may hold values from 0.019897461 to 0.5
- saved_acts: bfloat16 [8, 4, 16, 48, 1536], P('dp', None, 'expert'), may hold values from -8 to 8
- down_weight: bfloat16 [16, 4096, 768], P('expert', 'dp'), may hold values from -0.09375 to 0.09375
Outputs:
- pre_grads: bfloat16 [8, 4, 16, 48, 1536], P('dp', None, 'expert')
- down_grad: bfloat16 [16, 4096, 768], P('expert', 'dp')
- gate_grad: float32 [4096, 4], P(('dp', 'expert'))
The draws below stay inside these ranges and needn't reach their ends.
Inputs may be any that keep to these rules, and one draw needn't show every extreme that they name: `expert_ids`: each token names 4 different experts; among the 128 tokens of one device no expert is named by more than 48 tokens, a bound that some block reaches.
All inputs are finite; a program needn't handle non-finite values.
Results may differ from the reference program's by a relative error of at most 0.0057.
Values may be sent and summed in bfloat16 or wider, within the bound.
No kernel may reach another device: no remote copies, remote signals or barrier semaphores. Data moves between devices by JAX's collectives and lax.ppermute only.
A program may use at most 192 MiB of HBM per device.

```python
import math
import jax
import jax.numpy as jnp
import numpy as np
from jax import lax

D = 4096
FF_W = 768
TOPK = 4
EXPERTS = 16
TOK_DEV = 128
CAP = 48
TOKENS = 4096
N_DP = 8
N_EXPERT = 4


def levels(own_key, extent, cuts, low, high):
    def one(axis_at, shards_of):
        draws = jax.random.uniform(jax.random.fold_in(jax.random.fold_in(own_key, 6), axis_at), (shards_of,), jnp.float32, low / len(cuts), high / len(cuts))
        return jnp.repeat(jnp.exp(draws), extent[axis_at] // shards_of).reshape((-1,) + (1,) * (len(extent) - axis_at - 1))

    loudness = one(*cuts[0])
    for cut in cuts[1:]:
        loudness = loudness * one(*cut)
    return loudness


def shared_out(key, own, number, rows, amount, top, limit, lean):
    order = jax.random.permutation(key, amount)
    crowded, ordinary = shares(amount, rows * top, limit, lean, True), shares(amount, rows * top, limit, lean, False)
    places = jnp.arange(amount)

    def named(tallies, offset_by):
        used = int((tallies > 0).sum())
        fixed = max(1, used // 4)
        shifted = fixed + (places - fixed + offset_by * (used - fixed)) % max(1, amount - fixed)
        return jnp.zeros((amount,), jnp.int32).at[order[jnp.where(places < fixed, places, shifted)]].set(jnp.asarray(tallies, jnp.int32))

    tallies = jnp.where(number % 4 == 0, named(crowded, number // 4), named(ordinary, number - number // 4 - 1))
    mixed = jax.random.permutation(jax.random.fold_in(own, 3), amount)
    source_of, taker = mixed[0:amount // 2 * 2:2], mixed[1:amount // 2 * 2:2]
    margin = jnp.minimum(tallies[source_of] - 1, limit - tallies[taker]) // 2
    margin = jnp.where((source_of == order[0]) | (taker == order[0]) | (tallies[taker] == 0), 0, jnp.maximum(margin, 0))
    shifted = jax.random.randint(jax.random.fold_in(own, 4), (amount // 2,), 0, 1 << 20) % (margin + 1)
    tallies = tallies.at[source_of].add(-shifted).at[taker].add(shifted)
    items = jnp.searchsorted(jnp.cumsum(tallies), jnp.arange(rows * top), side="right").astype(jnp.int32)
    listing = items.reshape(top, rows).T
    listing = listing[jax.random.permutation(jax.random.fold_in(own, 1), rows)]
    offset_by = jax.random.randint(jax.random.fold_in(own, 2), (rows, 1), 0, top)
    return jnp.take_along_axis(listing, (jnp.arange(top)[None, :] + offset_by) % top, axis=1)


def shares(number_of, total, reach, skew, full):
    loads = [(1 << 20) // math.isqrt(standing ** skew) + 1 for standing in range(1, number_of + 1)]
    largest = reach if full else min(reach, max(-(-total // number_of), total * loads[0] // sum(loads)))
    least = 1 if total - largest >= number_of - 1 else 0
    counts, rest = [largest] + [least] * (number_of - 1), total - largest - least * (number_of - 1)
    while rest > 0:
        candidates = [i for i in range(1, number_of) if counts[i] < largest] or [i for i in range(1, number_of) if counts[i] < reach]
        pool, left = sum([loads[i] for i in candidates]), rest
        for i in candidates:
            extra = min(reach - counts[i], max(1, left * loads[i] // pool), rest)
            counts[i] = counts[i] + extra
            rest = rest - extra
    return np.array(counts)


def bell_draw(stream_key, dims, deviation, reach, pieces=(), kind=jnp.bfloat16):
    factor_of = levels(stream_key, dims, pieces, -0.22, 0.18) if pieces else 1.0
    array = jax.random.normal(stream_key, dims, jnp.float32) * deviation * factor_of
    return jnp.minimum(jnp.maximum(array, -reach), reach).astype(kind)


def setup_inputs(seed: int = 0) -> dict:
    streams_of = jax.random.split(jax.random.key(seed), 6)
    out_grad = bell_draw(streams_of[0], (TOKENS, D), 1.0, 6.0, ((0, 32),))
    expert_ids_keys = jax.random.split(jax.random.fold_in(streams_of[1], 1), TOKENS // TOK_DEV)
    expert_ids_turns = jax.random.permutation(jax.random.fold_in(streams_of[1], 3), TOKENS // TOK_DEV)
    expert_ids = jax.vmap(lambda own, number: shared_out(jax.random.fold_in(streams_of[1], 2), own, number, TOK_DEV, EXPERTS, TOPK, CAP, 2))(expert_ids_keys, expert_ids_turns).reshape((TOKENS, TOPK))
    gate_weights = jnp.clip(jnp.exp(math.log(0.5) - 3.224016 * jax.random.uniform(streams_of[2], (TOKENS, TOPK), jnp.float32) ** levels(streams_of[2], (TOKENS, TOPK), ((0, 32),), -0.2, 0.2)), 0.019897461, 0.5).astype(jnp.bfloat16)
    saved_acts = bell_draw(streams_of[3], (N_DP, N_EXPERT, EXPERTS, CAP, 2 * FF_W), 1.5, 8.0, ((0, 8), (2, 4)))
    down_weight = bell_draw(streams_of[4], (EXPERTS, D, FF_W), D ** -0.5, 0.09375, ((0, 4), (1, 8)))
    return dict(out_grad=out_grad, expert_ids=expert_ids, gate_weights=gate_weights, saved_acts=saved_acts, down_weight=down_weight)


def slot_numbers(choice_rows):
    hits = jnp.sum((choice_rows[:, :, None] == jnp.arange(EXPERTS, dtype=jnp.int32)[None, None, :]).astype(jnp.int32), axis=1)
    before = (jnp.cumsum(hits, axis=0) - hits).astype(jnp.int32)
    return jnp.take_along_axis(before, choice_rows, axis=1).astype(jnp.int32)


def reference(out_grad, expert_ids, gate_weights, saved_acts, down_weight):
    sources = N_EXPERT
    grads = out_grad.reshape(N_DP, sources, TOK_DEV, D)
    choice_rows = expert_ids.reshape(N_DP, sources, TOK_DEV, TOPK)
    gates = gate_weights.reshape(N_DP, sources, TOK_DEV, TOPK)
    weight_f = down_weight.astype(jnp.float32)
    total_slots = sources * EXPERTS * CAP

    def one_group(carry, group):
        grad_row, id_row, gate_row, saved_row = group
        slots = jax.vmap(slot_numbers)(id_row)
        source_index = lax.broadcasted_iota(jnp.int32, id_row.shape, 0)
        target = ((source_index * EXPERTS + id_row) * CAP + slots).astype(jnp.int32)
        flat_target = target.reshape(-1)
        copies = jnp.broadcast_to(grad_row[:, :, None, :], id_row.shape + (D,)).reshape(-1, D)
        routed = jnp.zeros((total_slots, D), jnp.bfloat16).at[flat_target].set(copies).reshape(sources, EXPERTS, CAP, D)
        gate_slot = jnp.zeros((total_slots,), jnp.float32).at[flat_target].set(gate_row.reshape(-1).astype(jnp.float32)).reshape(sources, EXPERTS, CAP)
        gate_pre = saved_row[..., :FF_W].astype(jnp.float32)
        up_pre = saved_row[..., FF_W:].astype(jnp.float32)
        sigma = jax.nn.sigmoid(gate_pre)
        silu_val = gate_pre * sigma
        act = silu_val * up_pre
        back = jnp.einsum("secd,edf->secf", routed.astype(jnp.float32), weight_f)
        score = jnp.sum(back * act, axis=3)
        grad_act = gate_slot[..., None] * back
        d_gate = grad_act * up_pre * sigma * (1.0 + gate_pre * (1.0 - sigma))
        d_up = grad_act * silu_val
        pre_grad = jnp.concatenate([d_gate, d_up], axis=3).astype(jnp.bfloat16)
        act_low = act.astype(jnp.bfloat16)
        weighted = (gate_slot[..., None] * routed.astype(jnp.float32)).astype(jnp.bfloat16)
        share = jnp.einsum("secd,secf->edf", weighted.astype(jnp.float32), act_low.astype(jnp.float32))
        gate_row_grad = score.reshape(-1)[flat_target].reshape(id_row.shape)
        return carry + share, (pre_grad, gate_row_grad)

    start_sum = jnp.zeros((EXPERTS, D, FF_W), jnp.float32)
    summed, (pre_grads, gate_grad) = lax.scan(one_group, start_sum, (grads, choice_rows, gates, saved_acts))
    return pre_grads, summed.astype(jnp.bfloat16), gate_grad.reshape(TOKENS, TOPK)
```

```python
import functools

import jax
import jax.numpy as jnp
from jax import lax
from jax.experimental import pallas as pl
from jax.experimental.pallas import tpu as pltpu
from jax.sharding import PartitionSpec as P

EXPERTS = 16
CAP = 48
META = 16
NONE = 255.0
BF = jnp.bfloat16
F32 = jnp.float32


def params(mib):
    return pltpu.CompilerParams(vmem_limit_bytes=mib * 1024 * 1024)


def dot(a, b):
    return jnp.dot(a, b, preferred_element_type=F32)


def dot_t(a, b):
    return lax.dot_general(a, b, (((0,), (0,)), ((), ())), preferred_element_type=F32)


def named(ids, rows):
    experts = lax.broadcasted_iota(jnp.int32, (rows, EXPERTS), 1)
    return [(ids[:, k : k + 1] == experts).astype(F32) for k in range(ids.shape[1])]


def pack_kernel(rows, part, idx, grad_ref, ids_ref, gates_ref, *outs):
    cols = named(ids_ref[...], rows)
    gates = gates_ref[...].astype(F32)
    hit = sum(cols)
    gate = sum(c * gates[:, k : k + 1] for k, c in enumerate(cols))
    r = lax.broadcasted_iota(jnp.int32, (rows, rows), 0)
    c = lax.broadcasted_iota(jnp.int32, (rows, rows), 1)
    earlier, eye = (r < c).astype(BF), (r == c).astype(BF)
    before = dot_t(hit.astype(BF), earlier)
    hit_t = dot_t(hit.astype(BF), eye)
    gate_t = dot_t(gate.astype(BF), eye)
    slots = jnp.where(hit_t > 0.5, before, NONE)
    z = idx[0]
    for k, out in enumerate(outs):
        at = pl.multiple_of((z ^ k) * part, 128)
        out[0:rows, :] = grad_ref[:, pl.ds(at, part)]
        out[rows : rows + META, :] = jnp.zeros((META, part), BF)
        out[rows : rows + META, 0:rows] = slots.astype(BF)
        out[rows : rows + META, rows : 2 * rows] = gate_t.astype(BF)


def act_kernel(half, idx, saved_ref, keep_ref, send_ref):
    x = idx[1]
    width = 2 * half
    for out, side in ((send_ref, 1 - x), (keep_ref, x)):
        at = pl.multiple_of(side * half, 128)
        for e in range(saved_ref.shape[2]):
            g = saved_ref[0, 0, e, :, pl.ds(at, half)].astype(F32)
            u = saved_ref[0, 0, e, :, pl.ds(pl.multiple_of(width + at, 128), half)].astype(F32)
            out[e] = (g * lax.logistic(g) * u).astype(BF)


def pick(meta, row):
    rows = lax.broadcasted_iota(jnp.int32, meta.shape, 0)
    return jnp.sum(jnp.where(rows == row, meta, 0.0), axis=0, keepdims=True)


def spread(meta, expert, rows):
    line = pick(meta, expert)
    slots = lax.broadcasted_iota(jnp.int32, (CAP, rows), 0).astype(F32)
    hot = slots == line[:, 0:rows]
    return hot, jnp.where(hot, line[:, rows : 2 * rows], 0.0)


def route_kernel(rows, places, idx, a_ref, b_ref, own_ref, other_ref, part_ref, weighted_ref, routed):
    x, m = idx[1], idx[2]
    expert = m * pl.num_programs(0) + pl.program_id(0)
    near = a_ref.shape[0]
    sources = len(places) // 2
    for at, (jx, jm) in enumerate(places):
        ref, i = (a_ref, at) if at < near else (b_ref, at - near)
        meta = ref[i, rows : rows + META, 0 : 2 * rows].astype(F32)
        hot, gated = spread(meta, expert, rows)
        both = jnp.concatenate([hot.astype(BF), gated.astype(BF)], axis=0)
        got = dot(both, ref[i, 0:rows, :]).astype(BF)
        row = (jx * sources + jm) * CAP
        routed[row : row + CAP, :] = got[0:CAP]
        weighted_ref[0, row : row + CAP, :] = got[CAP:]
    depth = own_ref.shape[1]
    mine = pl.ds(pl.multiple_of(x * depth, 128), depth)
    theirs = pl.ds(pl.multiple_of((1 - x) * depth, 128), depth)
    back = dot(routed[:, mine], own_ref[0]) + dot(routed[:, theirs], other_ref[0])
    size = sources * CAP
    part_ref[0, 0] = back[0:size].astype(part_ref.dtype)
    part_ref[1, 0] = back[size:].astype(part_ref.dtype)


def grad_kernel(rows_of, idx, *refs):
    total = refs[-1]
    keep_ref, send_ref = refs[-3], refs[-2]
    refs = list(refs[:-3])
    z, x = idx[0], idx[1]
    nz = len(rows_of)
    outer = (z == 0) | (z == nz - 1)
    size = refs[0].shape[1] // 2
    acc = None
    for k, count in enumerate(rows_of):
        weighted = refs.pop(0)
        acts = [refs.pop(0) for _ in range(count)]
        for jx in range(2):
            act = acts[0][jx, 0]
            if count == 2:
                act = jnp.where(outer, act, acts[1][jx, 0])
            term = dot_t(weighted[0, jx * size : (jx + 1) * size, :], act)
            acc = term if acc is None else acc + term
    total[...] = acc
    depth = total.shape[0] // 2
    keep_ref[0] = total[pl.ds(pl.multiple_of(x * depth, 8), depth), :].astype(BF)
    send_ref[0] = total[pl.ds(pl.multiple_of((1 - x) * depth, 8), depth), :].astype(BF)


def last_kernel(rows, half, n_own, idx, saved_ref, meta_ref, *refs):
    owns, (other_ref, pre_ref, score_ref) = refs[:n_own], refs[n_own:]
    x, m = idx[1], idx[2]
    count = saved_ref.shape[2]
    width = 2 * half
    meta = meta_ref[0].astype(F32)
    r = lax.broadcasted_iota(jnp.int32, (CAP, 128), 0)
    c = lax.broadcasted_iota(jnp.int32, (CAP, 128), 1)
    for e in range(count):
        _, gated = spread(meta, m * count + e, rows)
        gate = jnp.sum(gated, axis=1, keepdims=True)
        score = jnp.zeros((CAP, 1), F32)
        for mine in (True, False):
            at = pl.multiple_of((x if mine else 1 - x) * half, 128)
            up_at = pl.multiple_of(width + at, 128)
            if mine:
                back = sum(o[0, e].astype(F32) for o in owns)
            else:
                back = other_ref[e].astype(F32)
            g = saved_ref[0, 0, e, :, pl.ds(at, half)].astype(F32)
            u = saved_ref[0, 0, e, :, pl.ds(up_at, half)].astype(F32)
            sig = lax.logistic(g)
            silu = g * sig
            score = score + jnp.sum(back * (silu * u), axis=1, keepdims=True)
            grad = gate * back
            pre_ref[0, 0, e, :, pl.ds(at, half)] = (grad * u * sig * (1.0 + g * (1.0 - sig))).astype(BF)
            pre_ref[0, 0, e, :, pl.ds(up_at, half)] = (grad * silu).astype(BF)
        score_ref[0, e : e + 1, :] = jnp.sum(jnp.where(r == c, score, 0.0), axis=0, keepdims=True)


def gate_kernel(rows, idx, ids_ref, *refs):
    out_ref = refs[-1]
    m = idx[2]
    cols = named(ids_ref[...], rows)
    r = lax.broadcasted_iota(jnp.int32, (rows, rows), 0)
    c = lax.broadcasted_iota(jnp.int32, (rows, rows), 1)
    before = dot((c < r).astype(BF), sum(cols).astype(BF))
    lanes = lax.broadcasted_iota(jnp.int32, (rows, 128), 1).astype(F32)
    at = lax.broadcasted_iota(jnp.int32, (rows, EXPERTS), 1)
    slots = [jnp.sum(col * before, axis=1, keepdims=True) for col in cols]
    names = [jnp.sum(jnp.where(col > 0.5, at, 0), axis=1, keepdims=True) for col in cols]
    outs = [jnp.zeros((rows, 1), F32) for _ in cols]
    for jm, ref in enumerate(refs[:-1]):
        for e in range(ref.shape[0]):
            expert = (m ^ jm) * ref.shape[0] + e
            line = ref[e : e + 1, :]
            for k in range(len(cols)):
                hit = (lanes == slots[k]) & (names[k] == expert)
                outs[k] = outs[k] + jnp.sum(jnp.where(hit, line, 0.0), axis=1, keepdims=True)
    for k, o in enumerate(outs):
        out_ref[:, k : k + 1] = o


def call(kernel, grid, in_specs, out_specs, out_shape, scratch=(), mib=32, cost=None):
    return pl.pallas_call(
        kernel,
        grid_spec=pltpu.PrefetchScalarGridSpec(
            num_scalar_prefetch=1,
            grid=grid,
            in_specs=in_specs,
            out_specs=out_specs,
            scratch_shapes=list(scratch),
        ),
        out_shape=out_shape,
        compiler_params=params(mib),
        cost_estimate=cost,
    )


def whole(shape):
    return pl.BlockSpec(shape, lambda *_: (0,) * len(shape))


def shards(out_grad, expert_ids, gate_weights, saved_acts, down_weight):
    sources = lax.axis_size("expert")
    n_dp = lax.axis_size("dp")
    nz = n_dp // 2
    line = nz == 4
    count, depth, width = down_weight.shape
    half = width // 2
    rows, model = out_grad.shape
    part = model // nz
    top = expert_ids.shape[1]
    size = sources * CAP
    dp, m = lax.axis_index("dp"), lax.axis_index("expert")
    z, x = dp // 2, dp % 2
    idx = jnp.stack([z, x, m]).astype(jnp.int32)

    def move_z(v, pairs):
        return lax.ppermute(v, "dp", [(2 * a + i, 2 * b + i) for a, b in pairs for i in range(2)])

    def flip_z(v, k):
        return move_z(v, [(a, a ^ k) for a in range(nz)])

    def flip_x(v):
        return lax.ppermute(v, "dp", [(i, i ^ 1) for i in range(n_dp)])

    def flip_m(v, k):
        return lax.ppermute(v, "expert", [(i, i ^ k) for i in range(sources)])

    pieces = call(
        functools.partial(pack_kernel, rows, part),
        (1,),
        [whole((rows, model)), whole((rows, top)), whole((rows, top))],
        [whole((rows + META, part))] * nz,
        [jax.ShapeDtypeStruct((rows + META, part), BF)] * nz,
    )(idx, out_grad, expert_ids, gate_weights)

    other_half = lax.dynamic_slice_in_dim(down_weight, (1 - x) * half, half, 2)
    own_w = lax.dynamic_slice_in_dim(down_weight, x * half, half, 2)
    other_w = flip_x(other_half)

    bits = []
    bit = sources // 2
    while bit:
        bits.append(bit)
        bit //= 2
    places = [(0, 0), (1, 0)]
    for bit in bits:
        places = places + [(jx, jm ^ bit) for jx, jm in places]

    near, far = {}, {}
    for k in sorted(range(nz), reverse=True):
        v = pieces[k] if k == 0 else flip_z(pieces[k], k)
        v = v[None]
        got = flip_x(v)
        for bit in bits:
            v = jnp.concatenate([v, got], axis=0)
            got = flip_m(v, bit)
        near[k], far[k] = v, got

    act_shape = jax.ShapeDtypeStruct((count, size, half), BF)
    act_spec = pl.BlockSpec((count, CAP, half), lambda j, idx: (0, j, 0))
    saved_spec = pl.BlockSpec((1, 1, count, CAP, 2 * width), lambda j, idx: (0, idx[2] ^ j, 0, 0, 0))
    keep, send = call(
        functools.partial(act_kernel, half),
        (sources,),
        [saved_spec],
        [act_spec, act_spec],
        [act_shape, act_shape],
    )(idx, saved_acts)
    own_act = jnp.stack([keep, flip_x(send)])

    inner = [(1, 2), (2, 1)]
    inward = [(0, 1), (3, 2)]
    outward = [(1, 0), (2, 3)]
    if line:
        r1 = flip_z(own_act, 1)
        i3 = move_z(own_act, inner)
        o2 = move_z(i3, outward)
        i2 = move_z(r1, inner)
        o3 = move_z(i2, outward)
        acts = [[own_act], [r1], [o2, i2], [o3, i3]]
    else:
        acts = [[own_act]] + [[flip_z(own_act, k)] for k in range(1, nz)]

    nb = len(places)
    blocks = pl.BlockSpec((nb // 2, rows + META, part), lambda e, idx: (0, 0, 0))
    w_spec = pl.BlockSpec((1, depth, half), lambda e, idx: (e, 0, 0))
    parts, weighted = {}, {}
    for k in sorted(range(nz), reverse=True):
        wire = k == nz - 1 or not line
        parts[k], weighted[k] = call(
            functools.partial(route_kernel, rows, places),
            (count,),
            [blocks, blocks, w_spec, w_spec],
            [
                pl.BlockSpec((2, 1, size, half), lambda e, idx: (0, e, 0, 0)),
                pl.BlockSpec((1, 2 * size, part), lambda e, idx: (e, 0, 0)),
            ],
            [
                jax.ShapeDtypeStruct((2, count, size, half), BF if wire and k else F32),
                jax.ShapeDtypeStruct((count, 2 * size, part), BF),
            ],
            [pltpu.VMEM((2 * size, part), BF)],
        )(idx, near[k], far[k], own_w, other_w)

    def plus(v, got):
        return (v + got.astype(F32)).astype(BF)

    if line:
        s1 = move_z(parts[3], inward)
        v2 = plus(parts[2], s1)
        s2_in = move_z(v2, inward)
        s2_mid = move_z(v2, inner)
        v3 = plus(parts[1], s2_mid)
        v4 = plus(parts[3].astype(F32), s2_in)
        got = [flip_z(v3, 1), move_z(v4, inner)]
    else:
        got = [flip_z(parts[k], k) for k in range(1, nz)]
    owns = [parts[0]] + got
    outgoing = sum(o[1].astype(F32) for o in owns).astype(BF)
    other = flip_x(outgoing)

    flat = []
    specs = []
    for k in range(nz):
        flat.append(weighted[k])
        specs.append(pl.BlockSpec((1, 2 * size, part), lambda e, idx: (e, 0, 0)))
        for a in acts[k]:
            flat.append(a)
            specs.append(pl.BlockSpec((2, 1, size, half), lambda e, idx: (0, e, 0, 0)))
    g_spec = pl.BlockSpec((1, depth, half), lambda e, idx: (e, 0, 0))
    g_shape = jax.ShapeDtypeStruct((count, depth, half), BF)
    g_keep, g_send = call(
        functools.partial(grad_kernel, [len(a) for a in acts]),
        (count,),
        specs,
        [g_spec, g_spec],
        [g_shape, g_shape],
        [pltpu.VMEM((part, half), F32)],
        mib=60,
    )(idx, *flat)
    g_got = flip_x(g_send)
    down_grad = jnp.where(
        x == 0,
        jnp.concatenate([g_keep, g_got], axis=2),
        jnp.concatenate([g_got, g_keep], axis=2),
    )

    order = {jm: at for at, (jx, jm) in enumerate(places) if jx == 0}
    n_near = near[0].shape[0]

    def meta_of(jm):
        at = order[jm]
        ref, i = (near[0], at) if at < n_near else (far[0], at - n_near)
        return ref[i, rows:, 0 : 2 * rows]

    meta = jnp.stack([meta_of(jm) for jm in range(sources)])
    own_spec = pl.BlockSpec((1, count, CAP, half), lambda j, idx: (0, 0, j, 0))
    pre_grads, scores = call(
        functools.partial(last_kernel, rows, half, len(owns)),
        (sources,),
        [saved_spec, pl.BlockSpec((1, META, 2 * rows), lambda j, idx: (j, 0, 0))]
        + [own_spec] * len(owns)
        + [act_spec],
        [saved_spec, pl.BlockSpec((1, count, 128), lambda j, idx: (j, 0, 0))],
        [
            jax.ShapeDtypeStruct(saved_acts.shape, BF),
            jax.ShapeDtypeStruct((sources, count, 128), F32),
        ],
    )(idx, saved_acts, meta, *owns, other)
    returned = [scores[0]] + [flip_m(scores[j], j) for j in range(1, sources)]
    gate_grad = call(
        functools.partial(gate_kernel, rows),
        (1,),
        [whole((rows, top))] + [whole((count, 128))] * sources,
        whole((rows, top)),
        jax.ShapeDtypeStruct((rows, top), F32),
    )(idx, expert_ids, *returned)
    return (pre_grads, down_grad, gate_grad)


def solution(mesh):
    placed = (
        P(("dp", "expert"), None),
        P(("dp", "expert"), None),
        P(("dp", "expert"), None),
        P("dp", None, "expert", None, None),
        P("expert", "dp", None),
    )
    return jax.shard_map(
        shards,
        mesh=mesh,
        in_specs=placed,
        out_specs=(
            P("dp", None, "expert", None, None),
            P("expert", "dp", None),
            P(("dp", "expert"), None),
        ),
        check_vma=False,
    )
```

```python
import functools

import jax
import jax.numpy as jnp
from jax import lax
from jax.experimental import pallas as pl
from jax.experimental.pallas import tpu as pltpu
from jax.sharding import PartitionSpec as P

EXPERTS = 16
CAP = 48
META = 16
NONE = 255.0
BF = jnp.bfloat16
F32 = jnp.float32


def params(mib):
    return pltpu.CompilerParams(vmem_limit_bytes=mib * 1024 * 1024)


def dot(a, b):
    return jnp.dot(a, b, preferred_element_type=F32)


def dot_t(a, b):
    return lax.dot_general(a, b, (((0,), (0,)), ((), ())), preferred_element_type=F32)


def named(ids, rows):
    experts = lax.broadcasted_iota(jnp.int32, (rows, EXPERTS), 1)
    return [(ids[:, k : k + 1] == experts).astype(F32) for k in range(ids.shape[1])]


def pack_kernel(rows, part, idx, grad_ref, ids_ref, gates_ref, *outs):
    cols = named(ids_ref[...], rows)
    gates = gates_ref[...].astype(F32)
    hit = sum(cols)
    gate = sum(c * gates[:, k : k + 1] for k, c in enumerate(cols))
    r = lax.broadcasted_iota(jnp.int32, (rows, rows), 0)
    c = lax.broadcasted_iota(jnp.int32, (rows, rows), 1)
    earlier, eye = (r < c).astype(BF), (r == c).astype(BF)
    before = dot_t(hit.astype(BF), earlier)
    hit_t = dot_t(hit.astype(BF), eye)
    gate_t = dot_t(gate.astype(BF), eye)
    slots = jnp.where(hit_t > 0.5, before, NONE)
    z = idx[0]
    for k, out in enumerate(outs):
        at = pl.multiple_of((z ^ k) * part, 128)
        out[0:rows, :] = grad_ref[:, pl.ds(at, part)]
        out[rows : rows + META, :] = jnp.zeros((META, part), BF)
        out[rows : rows + META, 0:rows] = slots.astype(BF)
        out[rows : rows + META, rows : 2 * rows] = gate_t.astype(BF)


def act_kernel(half, idx, saved_ref, keep_ref, send_ref):
    x = idx[1]
    width = 2 * half
    for out, side in ((send_ref, 1 - x), (keep_ref, x)):
        at = pl.multiple_of(side * half, 128)
        for e in range(saved_ref.shape[2]):
            g = saved_ref[0, 0, e, :, pl.ds(at, half)].astype(F32)
            u = saved_ref[0, 0, e, :, pl.ds(pl.multiple_of(width + at, 128), half)].astype(F32)
            out[e] = (g * lax.logistic(g) * u).astype(BF)


def pair_kernel(keep_ref, got_ref, out_ref):
    both = jnp.concatenate([keep_ref[0], got_ref[0]], axis=0)
    out_ref[0] = both.astype(F32).T.astype(BF)


def pick(meta, row):
    rows = lax.broadcasted_iota(jnp.int32, meta.shape, 0)
    return jnp.sum(jnp.where(rows == row, meta, 0.0), axis=0, keepdims=True)


def spread(meta, expert, rows):
    line = pick(meta, expert)
    slots = lax.broadcasted_iota(jnp.int32, (CAP, rows), 0).astype(F32)
    hot = slots == line[:, 0:rows]
    return hot, jnp.where(hot, line[:, rows : 2 * rows], 0.0)


def route_kernel(
    rows, places, count, half, cut, idx, a_ref, b_ref, c_ref, own_ref, *refs
):
    others, (part_ref, weighted_ref, routed) = refs[:-3], refs[-3:]
    other = others[0][0]
    if len(others) == 2:
        other = jnp.where(pl.program_id(0) >= cut, others[1][0], other)
    x, m = idx[1], idx[2]
    expert = m * count + pl.program_id(0)
    lots = [(r, i) for r in (a_ref, b_ref, c_ref) for i in range(r.shape[0])]
    sources = len(places) // 2
    for at, (jx, jm) in enumerate(places):
        ref, i = lots[at]
        meta = ref[i, rows : rows + META, 0 : 2 * rows].astype(F32)
        hot, gated = spread(meta, expert, rows)
        both = jnp.concatenate([hot.astype(BF), gated.astype(BF)], axis=0)
        got = dot(both, ref[i, 0:rows, :]).astype(BF)
        row = (jx * sources + jm) * CAP
        routed[row : row + CAP, :] = got[0:CAP]
        weighted_ref[0, row : row + CAP, :] = got[CAP:]
    depth = own_ref.shape[1]
    mine = pl.ds(pl.multiple_of(x * depth, 128), depth)
    theirs = pl.ds(pl.multiple_of((1 - x) * depth, 128), depth)
    own = own_ref[0, :, pl.ds(pl.multiple_of(x * half, 128), half)]
    back = dot(routed[:, mine], own) + dot(routed[:, theirs], other)
    size = sources * CAP
    part_ref[0, 0] = back[0:size].astype(part_ref.dtype)
    part_ref[1, 0] = back[size:].astype(part_ref.dtype)


def grad_kernel(rows_of, idx, *refs):
    keep_ref, send_ref, total = refs[-3:]
    refs = list(refs[:-3])
    z, x = idx[0], idx[1]
    nz = len(rows_of)
    outer = (z == 0) | (z == nz - 1)
    weighted = [refs.pop(0) for _ in range(nz)]
    acts = []
    for count in rows_of:
        act = refs.pop(0)[0]
        acts.append(jnp.where(outer, act, refs.pop(0)[0]) if count == 2 else act)
    step = min(256, total.shape[0])
    for n in range(0, total.shape[0], step):
        acc = sum(dot(act, w[0, :, n : n + step]) for act, w in zip(acts, weighted))
        total[n : n + step, :] = acc.T.astype(BF)
    depth = total.shape[0] // 2
    keep_ref[0] = total[pl.ds(pl.multiple_of(x * depth, 16), depth), :]
    send_ref[0] = total[pl.ds(pl.multiple_of((1 - x) * depth, 16), depth), :]


def join_kernel(half, idx, keep_ref, got_ref, out_ref):
    x = idx[1]
    out_ref[0, :, pl.ds(pl.multiple_of(x * half, 128), half)] = keep_ref[0]
    out_ref[0, :, pl.ds(pl.multiple_of((1 - x) * half, 128), half)] = got_ref[0]


def last_kernel(rows, half, n_own, first, total, more, idx, saved_ref, meta_ref, *refs):
    owns, other_ref, (pre_ref, score_ref) = refs[:n_own], refs[n_own], refs[n_own + 1 + more :]
    x, m = idx[1], idx[2]
    count = saved_ref.shape[2]
    width = 2 * half
    meta = meta_ref[0].astype(F32)
    r = lax.broadcasted_iota(jnp.int32, (CAP, 128), 0)
    c = lax.broadcasted_iota(jnp.int32, (CAP, 128), 1)
    for e in range(count):
        _, gated = spread(meta, m * total + first + e, rows)
        gate = jnp.sum(gated, axis=1, keepdims=True)
        score = jnp.zeros((CAP, 1), F32)
        for mine in (True, False):
            at = pl.multiple_of((x if mine else 1 - x) * half, 128)
            up_at = pl.multiple_of(width + at, 128)
            if mine:
                back = sum(o[0, e].astype(F32) for o in owns)
            else:
                back = other_ref[e].astype(F32)
            g = saved_ref[0, 0, e, :, pl.ds(at, half)].astype(F32)
            u = saved_ref[0, 0, e, :, pl.ds(up_at, half)].astype(F32)
            sig = lax.logistic(g)
            silu = g * sig
            score = score + jnp.sum(back * (silu * u), axis=1, keepdims=True)
            grad = gate * back
            pre_ref[0, 0, e, :, pl.ds(at, half)] = (grad * u * sig * (1.0 + g * (1.0 - sig))).astype(BF)
            pre_ref[0, 0, e, :, pl.ds(up_at, half)] = (grad * silu).astype(BF)
        score_ref[0, e : e + 1, :] = jnp.sum(jnp.where(r == c, score, 0.0), axis=0, keepdims=True)


def gate_kernel(rows, idx, ids_ref, *refs):
    out_ref = refs[-1]
    m = idx[2]
    cols = named(ids_ref[...], rows)
    r = lax.broadcasted_iota(jnp.int32, (rows, rows), 0)
    c = lax.broadcasted_iota(jnp.int32, (rows, rows), 1)
    before = dot((c < r).astype(BF), sum(cols).astype(BF))
    lanes = lax.broadcasted_iota(jnp.int32, (rows, 128), 1).astype(F32)
    at = lax.broadcasted_iota(jnp.int32, (rows, EXPERTS), 1)
    slots = [jnp.sum(col * before, axis=1, keepdims=True) for col in cols]
    names = [jnp.sum(jnp.where(col > 0.5, at, 0), axis=1, keepdims=True) for col in cols]
    outs = [jnp.zeros((rows, 1), F32) for _ in cols]
    for jm, ref in enumerate(refs[:-1]):
        for e in range(ref.shape[0]):
            expert = (m ^ jm) * ref.shape[0] + e
            line = ref[e : e + 1, :]
            for k in range(len(cols)):
                hit = (lanes == slots[k]) & (names[k] == expert)
                outs[k] = outs[k] + jnp.sum(jnp.where(hit, line, 0.0), axis=1, keepdims=True)
    for k, o in enumerate(outs):
        out_ref[:, k : k + 1] = o


def call(name, kernel, grid, in_specs, out_specs, out_shape, scratch=(), mib=32, alias=None, flops=0, moved=0):
    return pl.pallas_call(
        kernel,
        name=name,
        grid_spec=pltpu.PrefetchScalarGridSpec(
            num_scalar_prefetch=1,
            grid=grid,
            in_specs=in_specs,
            out_specs=out_specs,
            scratch_shapes=list(scratch),
        ),
        out_shape=out_shape,
        compiler_params=params(mib),
        input_output_aliases=alias or {},
        cost_estimate=pl.CostEstimate(flops=flops, bytes_accessed=moved, transcendentals=0),
    )


def after(v, *deps):
    return lax.optimization_barrier((v, *deps))[0]


def whole(shape):
    return pl.BlockSpec(shape, lambda *_: (0,) * len(shape))


def shards(out_grad, expert_ids, gate_weights, saved_acts, down_weight):
    sources = lax.axis_size("expert")
    n_dp = lax.axis_size("dp")
    nz = n_dp // 2
    line = nz == 4
    count, depth, width = down_weight.shape
    half = width // 2
    rows, model = out_grad.shape
    part = model // nz
    top = expert_ids.shape[1]
    size = sources * CAP
    lots, per = 1, count
    cuts = 2 if count % 2 == 0 else 1
    cut = count // cuts
    dp, m = lax.axis_index("dp"), lax.axis_index("expert")
    z, x = dp // 2, dp % 2
    idx = jnp.stack([z, x, m]).astype(jnp.int32)

    def move_z(v, pairs, name):
        with jax.named_scope(name):
            return lax.ppermute(v, "dp", [(2 * a + i, 2 * b + i) for a, b in pairs for i in range(2)])

    def flip_z(v, k, name):
        return move_z(v, [(a, a ^ k) for a in range(nz)], name)

    def flip_x(v, name):
        with jax.named_scope(name):
            return lax.ppermute(v, "dp", [(i, i ^ 1) for i in range(n_dp)])

    def flip_m(v, k, name):
        with jax.named_scope(name):
            return lax.ppermute(v, "expert", [(i, i ^ k) for i in range(sources)])

    inner = [(1, 2), (2, 1)]
    inward = [(0, 1), (3, 2)]
    outward = [(1, 0), (2, 3)]

    act_shape = jax.ShapeDtypeStruct((count, size, half), BF)
    act_spec = pl.BlockSpec((count, CAP, half), lambda j, idx: (0, j, 0))
    saved_spec = pl.BlockSpec((1, 1, count, CAP, 2 * width), lambda j, idx: (0, idx[2] ^ j, 0, 0, 0))
    keep, send = call(
        "act",
        functools.partial(act_kernel, half),
        (sources,),
        [saved_spec],
        [act_spec, act_spec],
        [act_shape, act_shape],
    )(idx, saved_acts)

    pieces = call(
        "pack",
        functools.partial(pack_kernel, rows, part),
        (1,),
        [whole((rows, model)), whole((rows, top)), whole((rows, top))],
        [whole((rows + META, part))] * nz,
        [jax.ShapeDtypeStruct((rows + META, part), BF)] * nz,
    )(idx, out_grad, expert_ids, gate_weights)

    bits = []
    bit = sources // 2
    while bit:
        bits.append(bit)
        bit //= 2
    def order_of(steps):
        seen = [(0, 0)]
        for bit in steps:
            seen = seen + [(jx ^ (bit == 0), jm ^ bit) for jx, jm in seen]
        return seen

    steps = {k: [0, *bits] if k else [bits[0], 0, *bits[1:]] for k in range(nz)}
    places = {k: order_of(steps[k]) for k in range(nz)}
    nb = 2 * sources
    parts, weighted = {}, {}
    near, far = {}, {}

    def route(k):
        blocks = pl.BlockSpec((nb // 2, rows + META, part), lambda e, idx: (0, 0, 0))
        quarter = pl.BlockSpec((nb // 4, rows + META, part), lambda e, idx: (0, 0, 0))
        wire = k and (k == nz - 1 or not line)
        out = call(
            f"route{k}",
            functools.partial(route_kernel, rows, places[k], count, half, cut),
            (count,),
            [blocks, quarter, quarter, pl.BlockSpec((1, depth, width), lambda e, idx: (e, 0, 0))]
            + [
                pl.BlockSpec((1, depth, half), lambda e, idx, i=i: (jnp.clip(e - i * cut, 0, cut - 1), 0, 0))
                for i in range(cuts)
            ],
            [
                pl.BlockSpec((2, 1, size, half), lambda e, idx: (0, e, 0, 0)),
                pl.BlockSpec((1, 2 * size, part), lambda e, idx: (e, 0, 0)),
            ],
            [
                jax.ShapeDtypeStruct((2, count, size, half), BF if wire else F32),
                jax.ShapeDtypeStruct((count, 2 * size, part), BF),
            ],
            [pltpu.VMEM((2 * size, part), BF)],
        )(idx, near[k], *far[k], down_weight, *other_w)
        weighted[k] = out[1]
        return out[0]

    weights = [
        lax.dynamic_slice(down_weight, (h * cut, 0, (1 - x) * half), (cut, depth, half))
        for h in range(cuts)
    ]
    first = nz - 1
    come = {0: pieces[0], first: flip_z(pieces[first], first, f"rows{first}_z")}
    act_got = flip_x(send, "act_x")
    other_w = [flip_x(weights[0], "weight0_x")]
    flat_spec = pl.BlockSpec((1, size, half), lambda e: (e, 0, 0))
    pair_spec = pl.BlockSpec((1, half, 2 * size), lambda e: (e, 0, 0))
    own_act = pl.pallas_call(
        pair_kernel,
        name="pair",
        grid=(count,),
        in_specs=[flat_spec, flat_spec],
        out_specs=pair_spec,
        out_shape=jax.ShapeDtypeStruct((count, half, 2 * size), BF),
        compiler_params=params(32),
    )(keep, act_got)
    if line:
        r1 = flip_z(own_act, 1, "act_z_r1")
        i3 = move_z(after(own_act, come[3]), inner, "act_z_i3")
        come[1] = flip_z(after(pieces[1], r1), 1, "rows1_z")
    else:
        for k in range(first - 1, 0, -1):
            come[k] = flip_z(after(pieces[k], come[first]), k, f"rows{k}_z")
        acts = [[own_act]] + [[flip_z(own_act, k, f"act_z{k}")] for k in range(1, nz)]

    def plus(v, got):
        return (v.astype(F32) + got.astype(F32)).astype(BF)

    ties = {}

    chains = {"x": [], "y": []}

    def stage(k, at):
        bit = steps[k][at]
        link = "x" if bit == 0 else "y" if bit == bits[0] else "c"
        tied = [*chains.get(link, []), *ties.get((link, k), [])]
        if at == 0:
            v = after(come[k][None], *tied)
        else:
            v = jnp.concatenate([near[k], *(after(u, *tied) for u in far[k])], axis=0)
        sent = [v]
        if at == len(steps[k]) - 1:
            sent = [v[: v.shape[0] // 2], v[v.shape[0] // 2 :]]
        if bit == 0:
            far[k] = [flip_x(u, f"rows{k}_x") for u in sent]
        else:
            far[k] = [flip_m(u, bit, f"rows{k}_expert{bit}") for u in sent]
        near[k] = v
        if link in chains:
            chains[link] = [far[k][-1]]

    def rest(k, start):
        for at in range(start, len(steps[k])):
            stage(k, at)

    if line:
        stage(0, 0)
    stage(first, 0)
    come3_x = far[first][0]
    if line:
        come[2] = flip_z(after(pieces[2], come3_x), 2, "rows2_z")
        ties["y", 3] = [other_w[0]]
        ties["c", 3] = [r1, i3]
    if cuts > 1:
        other_w.append(flip_x(after(weights[1], other_w[0], come3_x), "weight1_x"))
        chains["x"] = [other_w[-1]]
    rest(first, 1)
    parts[first, 0] = route(first)
    if line:
        s1 = [move_z(parts[3, 0], inward, "back_s1")]
        ties["x", 2] = [parts[3, 0]]
        stage(2, 0)
        o2 = move_z(i3, outward, "act_z_o2")
        i2 = move_z(r1, inner, "act_z_i2")
        stage(1, 0)
        stage(0, 1)
        come1_x, come0_x = far[1][0], far[0][0]
        stage(2, 1)
        ties["c", 2] = [come1_x, come0_x, *s1, o2, i2]
        rest(2, 2)
        parts[2, 0] = route(2)
        v2 = [plus(parts[2, 0], s1[0])]
        s2_in = [move_z(v2[0], inward, "back_s2_in")]
        s2_mid = [move_z(v2[0], inner, "back_s2_mid")]
        stage(1, 1)
        o3 = move_z(after(i2, *s1), outward, "act_z_o3")
        ties["c", 1] = [parts[2, 0]]
        rest(1, 2)
        acts = [[own_act], [r1], [o2, i2], [o3, i3]]
        parts[1, 0] = route(1)
        ties["c", 0] = [*far[1]]
        rest(0, 2)
        near[0] = after(near[0], o3)
        parts[0, 0] = route(0)
    else:
        for k in range(first - 1, -1, -1):
            rest(k, 0)
            parts[k, 0] = route(k)

    flat = [weighted[k] for k in range(nz)]
    specs = [pl.BlockSpec((1, 2 * size, part), lambda e, idx: (e, 0, 0))] * nz
    for act in acts:
        flat += act
        specs += [pl.BlockSpec((1, half, 2 * size), lambda e, idx: (e, 0, 0))] * len(act)
    g_spec = pl.BlockSpec((1, depth, half), lambda e, idx: (e, 0, 0))
    g_shape = jax.ShapeDtypeStruct((count, depth, half), BF)
    g_keep, g_send = call(
        "down_grad",
        functools.partial(grad_kernel, [len(a) for a in acts]),
        (count,),
        specs,
        [g_spec, g_spec],
        [g_shape, g_shape],
        [pltpu.VMEM((part, half), BF)],
        mib=60,
        flops=2 * count * nz * 2 * size * part * half,
        moved=sum(v.size * 2 for v in flat),
    )(idx, *flat)
    if line:
        v3 = [plus(parts[1, h], s2_mid[h]) for h in range(lots)]
        v4 = [plus(parts[3, h], s2_in[h]) for h in range(lots)]
        v3[0] = after(v3[0], g_send)
        v4[0] = after(v4[0], g_send)
        got = [
            [flip_z(v3[h], 1, f"back{h}_s3_flip"), move_z(v4[h], inner, f"back{h}_s3_mid")]
            for h in range(lots)
        ]
    else:
        got = [[flip_z(parts[k, h], k, f"back{h}_{k}") for k in range(1, nz)] for h in range(lots)]
    owns = [[parts[0, h]] + got[h] for h in range(lots)]

    g_got = flip_x(g_send, "grad_x")
    down_grad = call(
        "join",
        functools.partial(join_kernel, half),
        (count,),
        [g_spec, g_spec],
        pl.BlockSpec((1, depth, width), lambda e, idx: (e, 0, 0)),
        jax.ShapeDtypeStruct((count, depth, width), BF),
    )(idx, g_keep, g_got)

    outgoing = [sum(o[1].astype(F32) for o in own).astype(BF) for own in owns]
    outgoing[0] = after(outgoing[0], g_send)
    other = [flip_x(outgoing[h], f"back{h}_x") for h in range(lots)]

    order = {jm: at for at, (jx, jm) in enumerate(places[0]) if jx == 0}
    blocks = [(v, i) for v in (near[0], *far[0]) for i in range(v.shape[0])]

    def meta_of(jm):
        ref, i = blocks[order[jm]]
        return ref[i, rows:, 0 : 2 * rows]

    meta = jnp.stack([meta_of(jm) for jm in range(sources)])
    own_spec = pl.BlockSpec((1, per, CAP, half), lambda j, idx: (0, 0, j, 0))
    pre_grads = None
    scores = []
    for h in range(lots):
        piece = pl.BlockSpec(
            (1, 1, per, CAP, 2 * width), lambda j, idx, h=h: (0, idx[2] ^ j, h, 0, 0)
        )
        pre_grads, score = call(
            f"owner{h}",
            functools.partial(last_kernel, rows, half, len(owns[h]), h * per, count, h > 0),
            (sources,),
            [piece, pl.BlockSpec((1, META, 2 * rows), lambda j, idx: (j, 0, 0))]
            + [own_spec] * len(owns[h])
            + [pl.BlockSpec((per, CAP, half), lambda j, idx: (0, j, 0))]
            + [pl.BlockSpec(memory_space=pl.ANY)] * (h > 0),
            [piece, pl.BlockSpec((1, per, 128), lambda j, idx: (j, 0, 0))],
            [
                jax.ShapeDtypeStruct(saved_acts.shape, BF),
                jax.ShapeDtypeStruct((sources, per, 128), F32),
            ],
            alias={len(owns[h]) + 4: 0} if h else {},
        )(idx, saved_acts, meta, *owns[h], other[h], *([pre_grads] if h else []))
        scores.append(score)
    scores = jnp.concatenate(scores, axis=1)
    returned = [scores[0]] + [flip_m(scores[j], j, f"score{j}") for j in range(1, sources)]
    gate_grad = call(
        "gate_grad",
        functools.partial(gate_kernel, rows),
        (1,),
        [whole((rows, top))] + [whole((count, 128))] * sources,
        whole((rows, top)),
        jax.ShapeDtypeStruct((rows, top), F32),
    )(idx, expert_ids, *returned)
    return (pre_grads, down_grad, gate_grad)


def solution(mesh):
    placed = (
        P(("dp", "expert"), None),
        P(("dp", "expert"), None),
        P(("dp", "expert"), None),
        P("dp", None, "expert", None, None),
        P("expert", "dp", None),
    )
    return jax.shard_map(
        shards,
        mesh=mesh,
        in_specs=placed,
        out_specs=(
            P("dp", None, "expert", None, None),
            P("expert", "dp", None),
            P(("dp", "expert"), None),
        ),
        check_vma=False,
    )
```

```python
import functools

import jax
import jax.numpy as jnp
from jax import lax
from jax.experimental import pallas as pl
from jax.experimental.pallas import tpu as pltpu
from jax.sharding import PartitionSpec as P

EXPERTS = 16
CAP = 48
META = 16
NONE = 255.0
BF = jnp.bfloat16
F32 = jnp.float32


def params(mib):
    return pltpu.CompilerParams(vmem_limit_bytes=mib * 1024 * 1024)


def dot(a, b):
    return jnp.dot(a, b, preferred_element_type=F32)


def dot_t(a, b):
    return lax.dot_general(a, b, (((0,), (0,)), ((), ())), preferred_element_type=F32)


def named(ids, rows):
    experts = lax.broadcasted_iota(jnp.int32, (rows, EXPERTS), 1)
    return [(ids[:, k : k + 1] == experts).astype(F32) for k in range(ids.shape[1])]


def pack_kernel(rows, part, idx, grad_ref, ids_ref, gates_ref, *outs):
    cols = named(ids_ref[...], rows)
    gates = gates_ref[...].astype(F32)
    hit = sum(cols)
    gate = sum(c * gates[:, k : k + 1] for k, c in enumerate(cols))
    r = lax.broadcasted_iota(jnp.int32, (rows, rows), 0)
    c = lax.broadcasted_iota(jnp.int32, (rows, rows), 1)
    earlier, eye = (r < c).astype(BF), (r == c).astype(BF)
    before = dot_t(hit.astype(BF), earlier)
    hit_t = dot_t(hit.astype(BF), eye)
    gate_t = dot_t(gate.astype(BF), eye)
    slots = jnp.where(hit_t > 0.5, before, NONE)
    z = idx[0]
    for k, out in enumerate(outs):
        at = pl.multiple_of((z ^ k) * part, 128)
        out[0:rows, :] = grad_ref[:, pl.ds(at, part)]
        out[rows : rows + META, :] = jnp.zeros((META, part), BF)
        out[rows : rows + META, 0:rows] = slots.astype(BF)
        out[rows : rows + META, rows : 2 * rows] = gate_t.astype(BF)


def act_kernel(half, idx, saved_ref, keep_ref, send_ref):
    x = idx[1]
    width = 2 * half
    for out, side in ((send_ref, 1 - x), (keep_ref, x)):
        at = pl.multiple_of(side * half, 128)
        for e in range(saved_ref.shape[2]):
            g = saved_ref[0, 0, e, :, pl.ds(at, half)].astype(F32)
            u = saved_ref[0, 0, e, :, pl.ds(pl.multiple_of(width + at, 128), half)].astype(F32)
            out[e] = (g * lax.logistic(g) * u).astype(BF)


def pair_kernel(keep_ref, got_ref, out_ref):
    both = jnp.concatenate([keep_ref[0], got_ref[0]], axis=0)
    out_ref[0] = both.astype(F32).T.astype(BF)


def pick(meta, row):
    rows = lax.broadcasted_iota(jnp.int32, meta.shape, 0)
    return jnp.sum(jnp.where(rows == row, meta, 0.0), axis=0, keepdims=True)


def spread(meta, expert, rows):
    line = pick(meta, expert)
    slots = lax.broadcasted_iota(jnp.int32, (CAP, rows), 0).astype(F32)
    hot = slots == line[:, 0:rows]
    return hot, jnp.where(hot, line[:, rows : 2 * rows], 0.0)


def route_kernel(
    rows, places, count, half, cut, idx, a_ref, b_ref, c_ref, own_ref, *refs
):
    others, (part_ref, weighted_ref, routed) = refs[:-3], refs[-3:]
    other = others[0][0]
    if len(others) == 2:
        other = jnp.where(pl.program_id(0) >= cut, others[1][0], other)
    x, m = idx[1], idx[2]
    expert = m * count + pl.program_id(0)
    lots = [(r, i) for r in (a_ref, b_ref, c_ref) for i in range(r.shape[0])]
    sources = len(places) // 2
    for at, (jx, jm) in enumerate(places):
        ref, i = lots[at]
        meta = ref[i, rows : rows + META, 0 : 2 * rows].astype(F32)
        hot, gated = spread(meta, expert, rows)
        both = jnp.concatenate([hot.astype(BF), gated.astype(BF)], axis=0)
        got = dot(both, ref[i, 0:rows, :]).astype(BF)
        row = (jx * sources + jm) * CAP
        routed[row : row + CAP, :] = got[0:CAP]
        weighted_ref[0, row : row + CAP, :] = got[CAP:]
    depth = own_ref.shape[1]
    mine = pl.ds(pl.multiple_of(x * depth, 128), depth)
    theirs = pl.ds(pl.multiple_of((1 - x) * depth, 128), depth)
    own = own_ref[0, :, pl.ds(pl.multiple_of(x * half, 128), half)]
    back = dot(routed[:, mine], own) + dot(routed[:, theirs], other)
    size = sources * CAP
    part_ref[0, 0] = back[0:size].astype(part_ref.dtype)
    part_ref[1, 0] = back[size:].astype(part_ref.dtype)


def grad_kernel(rows_of, idx, *refs):
    keep_ref, send_ref, total = refs[-3:]
    refs = list(refs[:-3])
    z, x = idx[0], idx[1]
    nz = len(rows_of)
    outer = (z == 0) | (z == nz - 1)
    weighted = [refs.pop(0) for _ in range(nz)]
    acts = []
    for count in rows_of:
        act = refs.pop(0)[0]
        acts.append(jnp.where(outer, act, refs.pop(0)[0]) if count == 2 else act)
    step = min(256, total.shape[0])
    for n in range(0, total.shape[0], step):
        acc = sum(dot(act, w[0, :, n : n + step]) for act, w in zip(acts, weighted))
        total[n : n + step, :] = acc.T.astype(BF)
    depth = total.shape[0] // 2
    keep_ref[0] = total[pl.ds(pl.multiple_of(x * depth, 16), depth), :]
    send_ref[0] = total[pl.ds(pl.multiple_of((1 - x) * depth, 16), depth), :]


def join_kernel(half, idx, keep_ref, got_ref, out_ref):
    x = idx[1]
    out_ref[0, :, pl.ds(pl.multiple_of(x * half, 128), half)] = keep_ref[0]
    out_ref[0, :, pl.ds(pl.multiple_of((1 - x) * half, 128), half)] = got_ref[0]


def last_kernel(rows, half, n_own, first, total, more, idx, saved_ref, meta_ref, *refs):
    owns, other_ref, (pre_ref, score_ref) = refs[:n_own], refs[n_own], refs[n_own + 1 + more :]
    x, m = idx[1], idx[2]
    count = saved_ref.shape[2]
    width = 2 * half
    meta = meta_ref[0].astype(F32)
    r = lax.broadcasted_iota(jnp.int32, (CAP, 128), 0)
    c = lax.broadcasted_iota(jnp.int32, (CAP, 128), 1)
    for e in range(count):
        _, gated = spread(meta, m * total + first + e, rows)
        gate = jnp.sum(gated, axis=1, keepdims=True)
        score = jnp.zeros((CAP, 1), F32)
        for mine in (True, False):
            at = pl.multiple_of((x if mine else 1 - x) * half, 128)
            up_at = pl.multiple_of(width + at, 128)
            if mine:
                back = sum(o[0, e].astype(F32) for o in owns)
            else:
                back = other_ref[e].astype(F32)
            g = saved_ref[0, 0, e, :, pl.ds(at, half)].astype(F32)
            u = saved_ref[0, 0, e, :, pl.ds(up_at, half)].astype(F32)
            sig = lax.logistic(g)
            silu = g * sig
            score = score + jnp.sum(back * (silu * u), axis=1, keepdims=True)
            grad = gate * back
            pre_ref[0, 0, e, :, pl.ds(at, half)] = (grad * u * sig * (1.0 + g * (1.0 - sig))).astype(BF)
            pre_ref[0, 0, e, :, pl.ds(up_at, half)] = (grad * silu).astype(BF)
        score_ref[0, e : e + 1, :] = jnp.sum(jnp.where(r == c, score, 0.0), axis=0, keepdims=True)


def gate_kernel(rows, idx, ids_ref, *refs):
    out_ref = refs[-1]
    m = idx[2]
    cols = named(ids_ref[...], rows)
    r = lax.broadcasted_iota(jnp.int32, (rows, rows), 0)
    c = lax.broadcasted_iota(jnp.int32, (rows, rows), 1)
    before = dot((c < r).astype(BF), sum(cols).astype(BF))
    lanes = lax.broadcasted_iota(jnp.int32, (rows, 128), 1).astype(F32)
    at = lax.broadcasted_iota(jnp.int32, (rows, EXPERTS), 1)
    slots = [jnp.sum(col * before, axis=1, keepdims=True) for col in cols]
    names = [jnp.sum(jnp.where(col > 0.5, at, 0), axis=1, keepdims=True) for col in cols]
    outs = [jnp.zeros((rows, 1), F32) for _ in cols]
    for jm, ref in enumerate(refs[:-1]):
        for e in range(ref.shape[0]):
            expert = (m ^ jm) * ref.shape[0] + e
            line = ref[e : e + 1, :]
            for k in range(len(cols)):
                hit = (lanes == slots[k]) & (names[k] == expert)
                outs[k] = outs[k] + jnp.sum(jnp.where(hit, line, 0.0), axis=1, keepdims=True)
    for k, o in enumerate(outs):
        out_ref[:, k : k + 1] = o


def call(name, kernel, grid, in_specs, out_specs, out_shape, scratch=(), mib=20, alias=None, flops=0, moved=0):
    return pl.pallas_call(
        kernel,
        name=name,
        grid_spec=pltpu.PrefetchScalarGridSpec(
            num_scalar_prefetch=1,
            grid=grid,
            in_specs=in_specs,
            out_specs=out_specs,
            scratch_shapes=list(scratch),
        ),
        out_shape=out_shape,
        compiler_params=params(mib),
        input_output_aliases=alias or {},
        cost_estimate=pl.CostEstimate(flops=flops, bytes_accessed=moved, transcendentals=0),
    )


def after(v, *deps):
    return lax.optimization_barrier((v, *deps))[0]


def whole(shape):
    return pl.BlockSpec(shape, lambda *_: (0,) * len(shape))


def shards(out_grad, expert_ids, gate_weights, saved_acts, down_weight):
    sources = lax.axis_size("expert")
    n_dp = lax.axis_size("dp")
    nz = n_dp // 2
    line = nz == 4
    count, depth, width = down_weight.shape
    half = width // 2
    rows, model = out_grad.shape
    part = model // nz
    top = expert_ids.shape[1]
    size = sources * CAP
    lots, per = 1, count
    cuts = 2 if count % 2 == 0 else 1
    cut = count // cuts
    dp, m = lax.axis_index("dp"), lax.axis_index("expert")
    z, x = dp // 2, dp % 2
    idx = jnp.stack([z, x, m]).astype(jnp.int32)

    def move_z(v, pairs, name):
        with jax.named_scope(name):
            return lax.ppermute(v, "dp", [(2 * a + i, 2 * b + i) for a, b in pairs for i in range(2)])

    def flip_z(v, k, name):
        return move_z(v, [(a, a ^ k) for a in range(nz)], name)

    def flip_x(v, name):
        with jax.named_scope(name):
            return lax.ppermute(v, "dp", [(i, i ^ 1) for i in range(n_dp)])

    def flip_m(v, k, name):
        with jax.named_scope(name):
            return lax.ppermute(v, "expert", [(i, i ^ k) for i in range(sources)])

    inner = [(1, 2), (2, 1)]
    inward = [(0, 1), (3, 2)]
    outward = [(1, 0), (2, 3)]

    act_shape = jax.ShapeDtypeStruct((count, size, half), BF)
    act_spec = pl.BlockSpec((count, CAP, half), lambda j, idx: (0, j, 0))
    saved_spec = pl.BlockSpec((1, 1, count, CAP, 2 * width), lambda j, idx: (0, idx[2] ^ j, 0, 0, 0))
    keep, send = call(
        "act",
        functools.partial(act_kernel, half),
        (sources,),
        [saved_spec],
        [act_spec, act_spec],
        [act_shape, act_shape],
    )(idx, saved_acts)

    pieces = call(
        "pack",
        functools.partial(pack_kernel, rows, part),
        (1,),
        [whole((rows, model)), whole((rows, top)), whole((rows, top))],
        [whole((rows + META, part))] * nz,
        [jax.ShapeDtypeStruct((rows + META, part), BF)] * nz,
    )(idx, out_grad, expert_ids, gate_weights)

    bits = []
    bit = sources // 2
    while bit:
        bits.append(bit)
        bit //= 2
    def order_of(steps):
        seen = [(0, 0)]
        for bit in steps:
            seen = seen + [(jx ^ (bit == 0), jm ^ bit) for jx, jm in seen]
        return seen

    steps = {k: [0, *bits] if k else [bits[0], 0, *bits[1:]] for k in range(nz)}
    places = {k: order_of(steps[k]) for k in range(nz)}
    nb = 2 * sources
    parts, weighted = {}, {}
    near, far = {}, {}

    def route(k):
        blocks = pl.BlockSpec((nb // 2, rows + META, part), lambda e, idx: (0, 0, 0))
        quarter = pl.BlockSpec((nb // 4, rows + META, part), lambda e, idx: (0, 0, 0))
        wire = k and (k == nz - 1 or not line)
        out = call(
            f"route{k}",
            functools.partial(route_kernel, rows, places[k], count, half, cut),
            (count,),
            [blocks, quarter, quarter, pl.BlockSpec((1, depth, width), lambda e, idx: (e, 0, 0))]
            + [
                pl.BlockSpec((1, depth, half), lambda e, idx, i=i: (jnp.clip(e - i * cut, 0, cut - 1), 0, 0))
                for i in range(cuts)
            ],
            [
                pl.BlockSpec((2, 1, size, half), lambda e, idx: (0, e, 0, 0)),
                pl.BlockSpec((1, 2 * size, part), lambda e, idx: (e, 0, 0)),
            ],
            [
                jax.ShapeDtypeStruct((2, count, size, half), BF if wire else F32),
                jax.ShapeDtypeStruct((count, 2 * size, part), BF),
            ],
            [pltpu.VMEM((2 * size, part), BF)],
            mib=20 if line else 48,
        )(idx, near[k], *far[k], down_weight, *other_w)
        weighted[k] = out[1]
        return out[0]

    weights = [
        lax.dynamic_slice(down_weight, (h * cut, 0, (1 - x) * half), (cut, depth, half))
        for h in range(cuts)
    ]
    first = nz - 1
    come = {0: pieces[0], first: flip_z(pieces[first], first, f"rows{first}_z")}
    act_got = flip_x(send, "act_x")
    other_w = [flip_x(weights[0], "weight0_x")]
    flat_spec = pl.BlockSpec((1, size, half), lambda e: (e, 0, 0))
    pair_spec = pl.BlockSpec((1, half, 2 * size), lambda e: (e, 0, 0))
    own_act = pl.pallas_call(
        pair_kernel,
        name="pair",
        grid=(count,),
        in_specs=[flat_spec, flat_spec],
        out_specs=pair_spec,
        out_shape=jax.ShapeDtypeStruct((count, half, 2 * size), BF),
        compiler_params=params(16),
    )(keep, act_got)
    if line:
        r1 = flip_z(own_act, 1, "act_z_r1")
        i3 = move_z(after(own_act, come[3]), inner, "act_z_i3")
        come[1] = flip_z(after(pieces[1], r1), 1, "rows1_z")
    else:
        for k in range(first - 1, 0, -1):
            come[k] = flip_z(after(pieces[k], come[first]), k, f"rows{k}_z")
        acts = [[own_act]] + [[flip_z(own_act, k, f"act_z{k}")] for k in range(1, nz)]

    def plus(v, got):
        return (v.astype(F32) + got.astype(F32)).astype(BF)

    ties = {}

    chains = {"x": [], "y": []}

    def stage(k, at):
        bit = steps[k][at]
        link = "x" if bit == 0 else "y" if bit == bits[0] else "c"
        tied = [*chains.get(link, []), *ties.get((link, k), [])]
        if at == 0:
            v = after(come[k][None], *tied)
        else:
            v = jnp.concatenate([near[k], *(after(u, *tied) for u in far[k])], axis=0)
        sent = [v]
        if at == len(steps[k]) - 1:
            sent = [v[: v.shape[0] // 2], v[v.shape[0] // 2 :]]
        if bit == 0:
            far[k] = [flip_x(u, f"rows{k}_x") for u in sent]
        else:
            far[k] = [flip_m(u, bit, f"rows{k}_expert{bit}") for u in sent]
        near[k] = v
        if link in chains:
            chains[link] = [far[k][-1]]

    def rest(k, start):
        for at in range(start, len(steps[k])):
            stage(k, at)

    if line:
        stage(0, 0)
    stage(first, 0)
    come3_x = far[first][0]
    if line:
        come[2] = flip_z(after(pieces[2], come3_x), 2, "rows2_z")
        ties["y", 3] = [other_w[0]]
        ties["c", 3] = [r1, i3]
    if cuts > 1:
        other_w.append(flip_x(after(weights[1], other_w[0], come3_x), "weight1_x"))
        chains["x"] = [other_w[-1]]
    rest(first, 1)
    parts[first, 0] = route(first)
    if line:
        s1 = [move_z(parts[3, 0], inward, "back_s1")]
        ties["x", 2] = [parts[3, 0]]
        stage(2, 0)
        o2 = move_z(i3, outward, "act_z_o2")
        i2 = move_z(r1, inner, "act_z_i2")
        stage(1, 0)
        stage(0, 1)
        come1_x, come0_x = far[1][0], far[0][0]
        stage(2, 1)
        ties["c", 2] = [come1_x, come0_x, *s1, o2, i2]
        rest(2, 2)
        parts[2, 0] = route(2)
        v2 = [plus(parts[2, 0], s1[0])]
        s2_in = [move_z(v2[0], inward, "back_s2_in")]
        s2_mid = [move_z(v2[0], inner, "back_s2_mid")]
        stage(1, 1)
        o3 = move_z(after(i2, *s1), outward, "act_z_o3")
        ties["c", 1] = [parts[2, 0]]
        rest(1, 2)
        acts = [[own_act], [r1], [o2, i2], [o3, i3]]
        parts[1, 0] = route(1)
        ties["c", 0] = [*far[1]]
        rest(0, 2)
        near[0] = after(near[0], o3)
        parts[0, 0] = route(0)
    else:
        for k in range(first - 1, -1, -1):
            rest(k, 0)
            parts[k, 0] = route(k)

    flat = [weighted[k] for k in range(nz)]
    specs = [pl.BlockSpec((1, 2 * size, part), lambda e, idx: (e, 0, 0))] * nz
    for act in acts:
        flat += act
        specs += [pl.BlockSpec((1, half, 2 * size), lambda e, idx: (e, 0, 0))] * len(act)
    g_spec = pl.BlockSpec((1, depth, half), lambda e, idx: (e, 0, 0))
    g_shape = jax.ShapeDtypeStruct((count, depth, half), BF)
    g_keep, g_send = call(
        "down_grad",
        functools.partial(grad_kernel, [len(a) for a in acts]),
        (count,),
        specs,
        [g_spec, g_spec],
        [g_shape, g_shape],
        [pltpu.VMEM((part, half), BF)],
        mib=22 if line else 60,
        flops=2 * count * nz * 2 * size * part * half,
        moved=sum(v.size * 2 for v in flat),
    )(idx, *flat)
    if line:
        v3 = [plus(parts[1, h], s2_mid[h]) for h in range(lots)]
        v4 = [plus(parts[3, h], s2_in[h]) for h in range(lots)]
        v3[0] = after(v3[0], g_send)
        v4[0] = after(v4[0], g_send)
        got = [
            [flip_z(v3[h], 1, f"back{h}_s3_flip"), move_z(v4[h], inner, f"back{h}_s3_mid")]
            for h in range(lots)
        ]
    else:
        got = [[flip_z(parts[k, h], k, f"back{h}_{k}") for k in range(1, nz)] for h in range(lots)]
    owns = [[parts[0, h]] + got[h] for h in range(lots)]

    g_got = flip_x(g_send, "grad_x")
    down_grad = call(
        "join",
        functools.partial(join_kernel, half),
        (count,),
        [g_spec, g_spec],
        pl.BlockSpec((1, depth, width), lambda e, idx: (e, 0, 0)),
        jax.ShapeDtypeStruct((count, depth, width), BF),
    )(idx, g_keep, g_got)

    outgoing = [sum(o[1].astype(F32) for o in own).astype(BF) for own in owns]
    outgoing[0] = after(outgoing[0], g_got)
    other = [flip_x(outgoing[h], f"back{h}_x") for h in range(lots)]

    order = {jm: at for at, (jx, jm) in enumerate(places[0]) if jx == 0}
    blocks = [(v, i) for v in (near[0], *far[0]) for i in range(v.shape[0])]

    def meta_of(jm):
        ref, i = blocks[order[jm]]
        return ref[i, rows:, 0 : 2 * rows]

    meta = jnp.stack([meta_of(jm) for jm in range(sources)])
    own_spec = pl.BlockSpec((1, per, CAP, half), lambda j, idx: (0, 0, j, 0))
    pre_grads = None
    scores = []
    for h in range(lots):
        piece = pl.BlockSpec(
            (1, 1, per, CAP, 2 * width), lambda j, idx, h=h: (0, idx[2] ^ j, h, 0, 0)
        )
        pre_grads, score = call(
            f"owner{h}",
            functools.partial(last_kernel, rows, half, len(owns[h]), h * per, count, h > 0),
            (sources,),
            [piece, pl.BlockSpec((1, META, 2 * rows), lambda j, idx: (j, 0, 0))]
            + [own_spec] * len(owns[h])
            + [pl.BlockSpec((per, CAP, half), lambda j, idx: (0, j, 0))]
            + [pl.BlockSpec(memory_space=pl.ANY)] * (h > 0),
            [piece, pl.BlockSpec((1, per, 128), lambda j, idx: (j, 0, 0))],
            [
                jax.ShapeDtypeStruct(saved_acts.shape, BF),
                jax.ShapeDtypeStruct((sources, per, 128), F32),
            ],
            alias={len(owns[h]) + 4: 0} if h else {},
        )(idx, saved_acts, meta, *owns[h], other[h], *([pre_grads] if h else []))
        scores.append(score)
    scores = jnp.concatenate(scores, axis=1)
    returned = [scores[0]] + [flip_m(scores[j], j, f"score{j}") for j in range(1, sources)]
    gate_grad = call(
        "gate_grad",
        functools.partial(gate_kernel, rows),
        (1,),
        [whole((rows, top))] + [whole((count, 128))] * sources,
        whole((rows, top)),
        jax.ShapeDtypeStruct((rows, top), F32),
    )(idx, expert_ids, *returned)
    return (pre_grads, down_grad, gate_grad)


def solution(mesh):
    placed = (
        P(("dp", "expert"), None),
        P(("dp", "expert"), None),
        P(("dp", "expert"), None),
        P("dp", None, "expert", None, None),
        P("expert", "dp", None),
    )
    return jax.shard_map(
        shards,
        mesh=mesh,
        in_specs=placed,
        out_specs=(
            P("dp", None, "expert", None, None),
            P("expert", "dp", None),
            P(("dp", "expert"), None),
        ),
        check_vma=False,
    )
```

```python
import functools

import jax
import jax.numpy as jnp
from jax import lax
from jax.experimental import pallas as pl
from jax.experimental.pallas import tpu as pltpu
from jax.sharding import PartitionSpec as P

EXPERTS = 16
CAP = 48
META = 16
NONE = 255.0
BF = jnp.bfloat16
F32 = jnp.float32


def params(mib):
    return pltpu.CompilerParams(vmem_limit_bytes=mib * 1024 * 1024)


def dot(a, b):
    return jnp.dot(a, b, preferred_element_type=F32)


def dot_t(a, b):
    return lax.dot_general(a, b, (((0,), (0,)), ((), ())), preferred_element_type=F32)


def named(ids, rows):
    experts = lax.broadcasted_iota(jnp.int32, (rows, EXPERTS), 1)
    return [(ids[:, k : k + 1] == experts).astype(F32) for k in range(ids.shape[1])]


def pack_kernel(rows, part, idx, grad_ref, ids_ref, gates_ref, *outs):
    cols = named(ids_ref[...], rows)
    gates = gates_ref[...].astype(F32)
    hit = sum(cols)
    gate = sum(c * gates[:, k : k + 1] for k, c in enumerate(cols))
    r = lax.broadcasted_iota(jnp.int32, (rows, rows), 0)
    c = lax.broadcasted_iota(jnp.int32, (rows, rows), 1)
    earlier, eye = (r < c).astype(BF), (r == c).astype(BF)
    before = dot_t(hit.astype(BF), earlier)
    hit_t = dot_t(hit.astype(BF), eye)
    gate_t = dot_t(gate.astype(BF), eye)
    slots = jnp.where(hit_t > 0.5, before, NONE)
    z = idx[0]
    for k, out in enumerate(outs):
        at = pl.multiple_of((z ^ k) * part, 128)
        out[0:rows, :] = grad_ref[:, pl.ds(at, part)]
        out[rows : rows + META, :] = jnp.zeros((META, part), BF)
        out[rows : rows + META, 0:rows] = slots.astype(BF)
        out[rows : rows + META, rows : 2 * rows] = gate_t.astype(BF)


def act_kernel(half, idx, saved_ref, keep_ref, send_ref):
    x = idx[1]
    width = 2 * half
    for out, side in ((send_ref, 1 - x), (keep_ref, x)):
        at = pl.multiple_of(side * half, 128)
        for e in range(saved_ref.shape[2]):
            g = saved_ref[0, 0, e, :, pl.ds(at, half)].astype(F32)
            u = saved_ref[0, 0, e, :, pl.ds(pl.multiple_of(width + at, 128), half)].astype(F32)
            out[e] = (g * lax.logistic(g) * u).astype(BF)


def pair_kernel(keep_ref, got_ref, out_ref):
    both = jnp.concatenate([keep_ref[0], got_ref[0]], axis=0)
    out_ref[0] = both.astype(F32).T.astype(BF)


def pick(meta, row):
    rows = lax.broadcasted_iota(jnp.int32, meta.shape, 0)
    return jnp.sum(jnp.where(rows == row, meta, 0.0), axis=0, keepdims=True)


def spread(meta, expert, rows):
    line = pick(meta, expert)
    slots = lax.broadcasted_iota(jnp.int32, (CAP, rows), 0).astype(F32)
    hot = slots == line[:, 0:rows]
    return hot, jnp.where(hot, line[:, rows : 2 * rows], 0.0)


def route_kernel(
    rows, places, count, half, cut, idx, a_ref, b_ref, c_ref, own_ref, *refs
):
    others, (part_ref, weighted_ref, routed) = refs[:-3], refs[-3:]
    other = others[0][0]
    if len(others) == 2:
        other = jnp.where(pl.program_id(0) >= cut, others[1][0], other)
    x, m = idx[1], idx[2]
    expert = m * count + pl.program_id(0)
    lots = [(r, i) for r in (a_ref, b_ref, c_ref) for i in range(r.shape[0])]
    sources = len(places) // 2
    for at, (jx, jm) in enumerate(places):
        ref, i = lots[at]
        meta = ref[i, rows : rows + META, 0 : 2 * rows].astype(F32)
        hot, gated = spread(meta, expert, rows)
        both = jnp.concatenate([hot.astype(BF), gated.astype(BF)], axis=0)
        got = dot(both, ref[i, 0:rows, :]).astype(BF)
        row = (jx * sources + jm) * CAP
        routed[row : row + CAP, :] = got[0:CAP]
        weighted_ref[0, row : row + CAP, :] = got[CAP:]
    depth = own_ref.shape[1]
    mine = pl.ds(pl.multiple_of(x * depth, 128), depth)
    theirs = pl.ds(pl.multiple_of((1 - x) * depth, 128), depth)
    own = own_ref[0, :, pl.ds(pl.multiple_of(x * half, 128), half)]
    back = dot(routed[:, mine], own) + dot(routed[:, theirs], other)
    size = sources * CAP
    part_ref[0, 0] = back[0:size].astype(part_ref.dtype)
    part_ref[1, 0] = back[size:].astype(part_ref.dtype)


def grad_kernel(rows_of, idx, *refs):
    keep_ref, send_ref, total = refs[-3:]
    refs = list(refs[:-3])
    z, x = idx[0], idx[1]
    nz = len(rows_of)
    outer = (z == 0) | (z == nz - 1)
    weighted = [refs.pop(0) for _ in range(nz)]
    acts = []
    for count in rows_of:
        act = refs.pop(0)[0]
        acts.append(jnp.where(outer, act, refs.pop(0)[0]) if count == 2 else act)
    step = min(256, total.shape[0])
    for n in range(0, total.shape[0], step):
        acc = sum(dot(act, w[0, :, n : n + step]) for act, w in zip(acts, weighted))
        total[n : n + step, :] = acc.T.astype(BF)
    depth = total.shape[0] // 2
    keep_ref[0] = total[pl.ds(pl.multiple_of(x * depth, 16), depth), :]
    send_ref[0] = total[pl.ds(pl.multiple_of((1 - x) * depth, 16), depth), :]


def join_kernel(half, idx, keep_ref, got_ref, out_ref):
    x = idx[1]
    out_ref[0, :, pl.ds(pl.multiple_of(x * half, 128), half)] = keep_ref[0]
    out_ref[0, :, pl.ds(pl.multiple_of((1 - x) * half, 128), half)] = got_ref[0]


def last_kernel(rows, half, n_own, first, total, more, idx, saved_ref, meta_ref, *refs):
    owns, other_ref, (pre_ref, score_ref) = refs[:n_own], refs[n_own], refs[n_own + 1 + more :]
    x, m = idx[1], idx[2]
    count = saved_ref.shape[2]
    width = 2 * half
    meta = meta_ref[0].astype(F32)
    r = lax.broadcasted_iota(jnp.int32, (CAP, 128), 0)
    c = lax.broadcasted_iota(jnp.int32, (CAP, 128), 1)
    for e in range(count):
        _, gated = spread(meta, m * total + first + e, rows)
        gate = jnp.sum(gated, axis=1, keepdims=True)
        score = jnp.zeros((CAP, 1), F32)
        for mine in (True, False):
            at = pl.multiple_of((x if mine else 1 - x) * half, 128)
            up_at = pl.multiple_of(width + at, 128)
            if mine:
                back = sum(o[0, e].astype(F32) for o in owns)
            else:
                back = other_ref[e].astype(F32)
            g = saved_ref[0, 0, e, :, pl.ds(at, half)].astype(F32)
            u = saved_ref[0, 0, e, :, pl.ds(up_at, half)].astype(F32)
            sig = lax.logistic(g)
            silu = g * sig
            score = score + jnp.sum(back * (silu * u), axis=1, keepdims=True)
            grad = gate * back
            pre_ref[0, 0, e, :, pl.ds(at, half)] = (grad * u * sig * (1.0 + g * (1.0 - sig))).astype(BF)
            pre_ref[0, 0, e, :, pl.ds(up_at, half)] = (grad * silu).astype(BF)
        score_ref[0, e : e + 1, :] = jnp.sum(jnp.where(r == c, score, 0.0), axis=0, keepdims=True)


def gate_kernel(rows, idx, ids_ref, *refs):
    out_ref = refs[-1]
    m = idx[2]
    cols = named(ids_ref[...], rows)
    r = lax.broadcasted_iota(jnp.int32, (rows, rows), 0)
    c = lax.broadcasted_iota(jnp.int32, (rows, rows), 1)
    before = dot((c < r).astype(BF), sum(cols).astype(BF))
    lanes = lax.broadcasted_iota(jnp.int32, (rows, 128), 1).astype(F32)
    at = lax.broadcasted_iota(jnp.int32, (rows, EXPERTS), 1)
    slots = [jnp.sum(col * before, axis=1, keepdims=True) for col in cols]
    names = [jnp.sum(jnp.where(col > 0.5, at, 0), axis=1, keepdims=True) for col in cols]
    outs = [jnp.zeros((rows, 1), F32) for _ in cols]
    for jm, ref in enumerate(refs[:-1]):
        for e in range(ref.shape[0]):
            expert = (m ^ jm) * ref.shape[0] + e
            line = ref[e : e + 1, :]
            for k in range(len(cols)):
                hit = (lanes == slots[k]) & (names[k] == expert)
                outs[k] = outs[k] + jnp.sum(jnp.where(hit, line, 0.0), axis=1, keepdims=True)
    for k, o in enumerate(outs):
        out_ref[:, k : k + 1] = o


def call(name, kernel, grid, in_specs, out_specs, out_shape, scratch=(), mib=20, alias=None, flops=0, moved=0):
    return pl.pallas_call(
        kernel,
        name=name,
        grid_spec=pltpu.PrefetchScalarGridSpec(
            num_scalar_prefetch=1,
            grid=grid,
            in_specs=in_specs,
            out_specs=out_specs,
            scratch_shapes=list(scratch),
        ),
        out_shape=out_shape,
        compiler_params=params(mib),
        input_output_aliases=alias or {},
        cost_estimate=pl.CostEstimate(flops=flops, bytes_accessed=moved, transcendentals=0),
    )


def after(v, *deps):
    return lax.optimization_barrier((v, *deps))[0]


def whole(shape):
    return pl.BlockSpec(shape, lambda *_: (0,) * len(shape))


def shards(out_grad, expert_ids, gate_weights, saved_acts, down_weight):
    sources = lax.axis_size("expert")
    n_dp = lax.axis_size("dp")
    nz = n_dp // 2
    line = nz == 4
    count, depth, width = down_weight.shape
    half = width // 2
    rows, model = out_grad.shape
    part = model // nz
    top = expert_ids.shape[1]
    size = sources * CAP
    lots, per = 1, count
    cuts = 2 if count % 2 == 0 else 1
    cut = count // cuts
    dp, m = lax.axis_index("dp"), lax.axis_index("expert")
    z, x = dp // 2, dp % 2
    idx = jnp.stack([z, x, m]).astype(jnp.int32)

    def move_z(v, pairs, name):
        with jax.named_scope(name):
            return lax.ppermute(v, "dp", [(2 * a + i, 2 * b + i) for a, b in pairs for i in range(2)])

    def flip_z(v, k, name):
        return move_z(v, [(a, a ^ k) for a in range(nz)], name)

    def flip_x(v, name):
        with jax.named_scope(name):
            return lax.ppermute(v, "dp", [(i, i ^ 1) for i in range(n_dp)])

    def flip_m(v, k, name):
        with jax.named_scope(name):
            return lax.ppermute(v, "expert", [(i, i ^ k) for i in range(sources)])

    inner = [(1, 2), (2, 1)]
    inward = [(0, 1), (3, 2)]
    outward = [(1, 0), (2, 3)]

    act_shape = jax.ShapeDtypeStruct((count, size, half), BF)
    act_spec = pl.BlockSpec((count, CAP, half), lambda j, idx: (0, j, 0))
    saved_spec = pl.BlockSpec((1, 1, count, CAP, 2 * width), lambda j, idx: (0, idx[2] ^ j, 0, 0, 0))
    keep, send = call(
        "act",
        functools.partial(act_kernel, half),
        (sources,),
        [saved_spec],
        [act_spec, act_spec],
        [act_shape, act_shape],
    )(idx, saved_acts)

    pieces = call(
        "pack",
        functools.partial(pack_kernel, rows, part),
        (1,),
        [whole((rows, model)), whole((rows, top)), whole((rows, top))],
        [whole((rows + META, part))] * nz,
        [jax.ShapeDtypeStruct((rows + META, part), BF)] * nz,
    )(idx, out_grad, expert_ids, gate_weights)

    bits = []
    bit = sources // 2
    while bit:
        bits.append(bit)
        bit //= 2
    def order_of(steps):
        seen = [(0, 0)]
        for bit in steps:
            seen = seen + [(jx ^ (bit == 0), jm ^ bit) for jx, jm in seen]
        return seen

    steps = {k: [0, *bits] if k else [bits[0], 0, *bits[1:]] for k in range(nz)}
    places = {k: order_of(steps[k]) for k in range(nz)}
    nb = 2 * sources
    parts, weighted = {}, {}
    near, far = {}, {}

    def route(k):
        blocks = pl.BlockSpec((nb // 2, rows + META, part), lambda e, idx: (0, 0, 0))
        quarter = pl.BlockSpec((nb // 4, rows + META, part), lambda e, idx: (0, 0, 0))
        wire = k and (k == nz - 1 or not line)
        out = call(
            f"route{k}",
            functools.partial(route_kernel, rows, places[k], count, half, cut),
            (count,),
            [blocks, quarter, quarter, pl.BlockSpec((1, depth, width), lambda e, idx: (e, 0, 0))]
            + [
                pl.BlockSpec((1, depth, half), lambda e, idx, i=i: (jnp.clip(e - i * cut, 0, cut - 1), 0, 0))
                for i in range(cuts)
            ],
            [
                pl.BlockSpec((2, 1, size, half), lambda e, idx: (0, e, 0, 0)),
                pl.BlockSpec((1, 2 * size, part), lambda e, idx: (e, 0, 0)),
            ],
            [
                jax.ShapeDtypeStruct((2, count, size, half), BF if wire else F32),
                jax.ShapeDtypeStruct((count, 2 * size, part), BF),
            ],
            [pltpu.VMEM((2 * size, part), BF)],
            mib=20 if line else 48,
        )(idx, near[k], *far[k], down_weight, *other_w)
        weighted[k] = out[1]
        return out[0]

    weights = [
        lax.dynamic_slice(down_weight, (h * cut, 0, (1 - x) * half), (cut, depth, half))
        for h in range(cuts)
    ]
    first = nz - 1
    come = {0: pieces[0], first: flip_z(pieces[first], first, f"rows{first}_z")}
    act_got = flip_x(send, "act_x")
    other_w = [flip_x(weights[0], "weight0_x")]
    flat_spec = pl.BlockSpec((1, size, half), lambda e: (e, 0, 0))
    pair_spec = pl.BlockSpec((1, half, 2 * size), lambda e: (e, 0, 0))
    own_act = pl.pallas_call(
        pair_kernel,
        name="pair",
        grid=(count,),
        in_specs=[flat_spec, flat_spec],
        out_specs=pair_spec,
        out_shape=jax.ShapeDtypeStruct((count, half, 2 * size), BF),
        compiler_params=params(16),
    )(keep, act_got)
    if line:
        r1 = flip_z(own_act, 1, "act_z_r1")
        i3 = move_z(after(own_act, come[3]), inner, "act_z_i3")
        come[1] = flip_z(after(pieces[1], r1), 1, "rows1_z")
    else:
        for k in range(first - 1, 0, -1):
            come[k] = flip_z(after(pieces[k], come[first]), k, f"rows{k}_z")
        acts = [[own_act]] + [[flip_z(own_act, k, f"act_z{k}")] for k in range(1, nz)]

    def plus(v, got):
        return (v.astype(F32) + got.astype(F32)).astype(BF)

    ties = {}

    chains = {"x": [], "y": []}

    def stage(k, at):
        bit = steps[k][at]
        link = "x" if bit == 0 else "y" if bit == bits[0] else "c"
        tied = [*chains.get(link, []), *ties.get((link, k), [])]
        if at == 0:
            v = after(come[k][None], *tied)
        else:
            v = jnp.concatenate([near[k], *(after(u, *tied) for u in far[k])], axis=0)
        sent = [v]
        if at == len(steps[k]) - 1:
            sent = [v[: v.shape[0] // 2], v[v.shape[0] // 2 :]]
        if bit == 0:
            far[k] = [flip_x(u, f"rows{k}_x") for u in sent]
        else:
            far[k] = [flip_m(u, bit, f"rows{k}_expert{bit}") for u in sent]
        near[k] = v
        if link in chains:
            chains[link] = [far[k][-1]]

    def rest(k, start):
        for at in range(start, len(steps[k])):
            stage(k, at)

    if line:
        stage(0, 0)
    stage(first, 0)
    come3_x = far[first][0]
    if line:
        come[2] = flip_z(after(pieces[2], come3_x), 2, "rows2_z")
        ties["y", 3] = [other_w[0]]
        ties["c", 3] = [r1, i3]
    if cuts > 1:
        other_w.append(flip_x(after(weights[1], other_w[0], come3_x), "weight1_x"))
        chains["x"] = [other_w[-1]]
    rest(first, 1)
    parts[first, 0] = route(first)
    if line:
        s1 = [move_z(parts[3, 0], inward, "back_s1")]
        ties["x", 2] = [parts[3, 0]]
        stage(2, 0)
        o2 = move_z(i3, outward, "act_z_o2")
        i2 = move_z(r1, inner, "act_z_i2")
        stage(1, 0)
        stage(0, 1)
        come1_x, come0_x = far[1][0], far[0][0]
        stage(2, 1)
        ties["c", 2] = [come1_x, come0_x, *s1]
        rest(2, 2)
        parts[2, 0] = route(2)
        v2 = [plus(parts[2, 0], s1[0])]
        s2_in = [move_z(v2[0], inward, "back_s2_in")]
        s2_mid = [move_z(v2[0], inner, "back_s2_mid")]
        stage(1, 1)
        o3 = move_z(after(i2, *s1), outward, "act_z_o3")
        ties["c", 1] = [parts[2, 0], o2, i2]
        rest(1, 2)
        acts = [[own_act], [r1], [o2, i2], [o3, i3]]
        parts[1, 0] = route(1)
        ties["c", 0] = [*far[1]]
        rest(0, 2)
        near[0] = after(near[0], o3)
        parts[0, 0] = route(0)
    else:
        for k in range(first - 1, -1, -1):
            rest(k, 0)
            parts[k, 0] = route(k)

    flat = [weighted[k] for k in range(nz)]
    specs = [pl.BlockSpec((1, 2 * size, part), lambda e, idx: (e, 0, 0))] * nz
    for act in acts:
        flat += act
        specs += [pl.BlockSpec((1, half, 2 * size), lambda e, idx: (e, 0, 0))] * len(act)
    g_spec = pl.BlockSpec((1, depth, half), lambda e, idx: (e, 0, 0))
    g_shape = jax.ShapeDtypeStruct((count, depth, half), BF)
    g_keep, g_send = call(
        "down_grad",
        functools.partial(grad_kernel, [len(a) for a in acts]),
        (count,),
        specs,
        [g_spec, g_spec],
        [g_shape, g_shape],
        [pltpu.VMEM((part, half), BF)],
        mib=22 if line else 60,
        flops=2 * count * nz * 2 * size * part * half,
        moved=sum(v.size * 2 for v in flat),
    )(idx, *flat)
    if line:
        v3 = [plus(parts[1, h], s2_mid[h]) for h in range(lots)]
        v4 = [plus(parts[3, h], s2_in[h]) for h in range(lots)]
        v3[0] = after(v3[0], g_send)
        v4[0] = after(v4[0], g_send)
        got = [
            [flip_z(v3[h], 1, f"back{h}_s3_flip"), move_z(v4[h], inner, f"back{h}_s3_mid")]
            for h in range(lots)
        ]
    else:
        got = [[flip_z(parts[k, h], k, f"back{h}_{k}") for k in range(1, nz)] for h in range(lots)]
    owns = [[parts[0, h]] + got[h] for h in range(lots)]

    g_got = flip_x(g_send, "grad_x")
    down_grad = call(
        "join",
        functools.partial(join_kernel, half),
        (count,),
        [g_spec, g_spec],
        pl.BlockSpec((1, depth, width), lambda e, idx: (e, 0, 0)),
        jax.ShapeDtypeStruct((count, depth, width), BF),
    )(idx, g_keep, g_got)

    outgoing = [sum(o[1].astype(F32) for o in own).astype(BF) for own in owns]
    outgoing[0] = after(outgoing[0], g_got)
    other = [flip_x(outgoing[h], f"back{h}_x") for h in range(lots)]

    order = {jm: at for at, (jx, jm) in enumerate(places[0]) if jx == 0}
    blocks = [(v, i) for v in (near[0], *far[0]) for i in range(v.shape[0])]

    def meta_of(jm):
        ref, i = blocks[order[jm]]
        return ref[i, rows:, 0 : 2 * rows]

    meta = jnp.stack([meta_of(jm) for jm in range(sources)])
    own_spec = pl.BlockSpec((1, per, CAP, half), lambda j, idx: (0, 0, j, 0))
    pre_grads = None
    scores = []
    for h in range(lots):
        piece = pl.BlockSpec(
            (1, 1, per, CAP, 2 * width), lambda j, idx, h=h: (0, idx[2] ^ j, h, 0, 0)
        )
        pre_grads, score = call(
            f"owner{h}",
            functools.partial(last_kernel, rows, half, len(owns[h]), h * per, count, h > 0),
            (sources,),
            [piece, pl.BlockSpec((1, META, 2 * rows), lambda j, idx: (j, 0, 0))]
            + [own_spec] * len(owns[h])
            + [pl.BlockSpec((per, CAP, half), lambda j, idx: (0, j, 0))]
            + [pl.BlockSpec(memory_space=pl.ANY)] * (h > 0),
            [piece, pl.BlockSpec((1, per, 128), lambda j, idx: (j, 0, 0))],
            [
                jax.ShapeDtypeStruct(saved_acts.shape, BF),
                jax.ShapeDtypeStruct((sources, per, 128), F32),
            ],
            alias={len(owns[h]) + 4: 0} if h else {},
        )(idx, saved_acts, meta, *owns[h], other[h], *([pre_grads] if h else []))
        scores.append(score)
    scores = jnp.concatenate(scores, axis=1)
    returned = [scores[0]] + [flip_m(scores[j], j, f"score{j}") for j in range(1, sources)]
    gate_grad = call(
        "gate_grad",
        functools.partial(gate_kernel, rows),
        (1,),
        [whole((rows, top))] + [whole((count, 128))] * sources,
        whole((rows, top)),
        jax.ShapeDtypeStruct((rows, top), F32),
    )(idx, expert_ids, *returned)
    return (pre_grads, down_grad, gate_grad)


def solution(mesh):
    placed = (
        P(("dp", "expert"), None),
        P(("dp", "expert"), None),
        P(("dp", "expert"), None),
        P("dp", None, "expert", None, None),
        P("expert", "dp", None),
    )
    return jax.shard_map(
        shards,
        mesh=mesh,
        in_specs=placed,
        out_specs=(
            P("dp", None, "expert", None, None),
            P("expert", "dp", None),
            P(("dp", "expert"), None),
        ),
        check_vma=False,
    )
```

```python
import functools

import jax
import jax.numpy as jnp
from jax import lax
from jax.experimental import pallas as pl
from jax.experimental.pallas import tpu as pltpu
from jax.sharding import PartitionSpec as P

EXPERTS = 16
CAP = 48
META = 16
NONE = 255.0
BF = jnp.bfloat16
F32 = jnp.float32


def params(mib):
    return pltpu.CompilerParams(vmem_limit_bytes=mib * 1024 * 1024)


def dot(a, b):
    return jnp.dot(a, b, preferred_element_type=F32)


def dot_t(a, b):
    return lax.dot_general(a, b, (((0,), (0,)), ((), ())), preferred_element_type=F32)


def named(ids, rows):
    experts = lax.broadcasted_iota(jnp.int32, (rows, EXPERTS), 1)
    return [(ids[:, k : k + 1] == experts).astype(F32) for k in range(ids.shape[1])]


def pack_kernel(rows, part, idx, grad_ref, ids_ref, gates_ref, *outs):
    cols = named(ids_ref[...], rows)
    gates = gates_ref[...].astype(F32)
    hit = sum(cols)
    gate = sum(c * gates[:, k : k + 1] for k, c in enumerate(cols))
    r = lax.broadcasted_iota(jnp.int32, (rows, rows), 0)
    c = lax.broadcasted_iota(jnp.int32, (rows, rows), 1)
    earlier, eye = (r < c).astype(BF), (r == c).astype(BF)
    before = dot_t(hit.astype(BF), earlier)
    hit_t = dot_t(hit.astype(BF), eye)
    gate_t = dot_t(gate.astype(BF), eye)
    slots = jnp.where(hit_t > 0.5, before, NONE)
    z = idx[0]
    for k, out in enumerate(outs):
        at = pl.multiple_of((z ^ k) * part, 128)
        out[0:rows, :] = grad_ref[:, pl.ds(at, part)]
        out[rows : rows + META, :] = jnp.zeros((META, part), BF)
        out[rows : rows + META, 0:rows] = slots.astype(BF)
        out[rows : rows + META, rows : 2 * rows] = gate_t.astype(BF)


def act_kernel(half, idx, saved_ref, keep_ref, send_ref):
    x = idx[1]
    width = 2 * half
    for out, side in ((send_ref, 1 - x), (keep_ref, x)):
        at = pl.multiple_of(side * half, 128)
        for e in range(saved_ref.shape[2]):
            g = saved_ref[0, 0, e, :, pl.ds(at, half)].astype(F32)
            u = saved_ref[0, 0, e, :, pl.ds(pl.multiple_of(width + at, 128), half)].astype(F32)
            out[e] = (g * lax.logistic(g) * u).astype(BF)


def pair_kernel(keep_ref, got_ref, out_ref):
    both = jnp.concatenate([keep_ref[0], got_ref[0]], axis=0)
    out_ref[0] = both.astype(F32).T.astype(BF)


def pick(meta, row):
    rows = lax.broadcasted_iota(jnp.int32, meta.shape, 0)
    return jnp.sum(jnp.where(rows == row, meta, 0.0), axis=0, keepdims=True)


def spread(meta, expert, rows):
    line = pick(meta, expert)
    slots = lax.broadcasted_iota(jnp.int32, (CAP, rows), 0).astype(F32)
    hot = slots == line[:, 0:rows]
    return hot, jnp.where(hot, line[:, rows : 2 * rows], 0.0)


def route_kernel(
    rows, places, count, half, cut, idx, a_ref, b_ref, c_ref, own_ref, *refs
):
    others, (part_ref, weighted_ref, routed) = refs[:-3], refs[-3:]
    other = others[0][0]
    if len(others) == 2:
        other = jnp.where(pl.program_id(0) >= cut, others[1][0], other)
    x, m = idx[1], idx[2]
    expert = m * count + pl.program_id(0)
    lots = [(r, i) for r in (a_ref, b_ref, c_ref) for i in range(r.shape[0])]
    sources = len(places) // 2
    for at, (jx, jm) in enumerate(places):
        ref, i = lots[at]
        meta = ref[i, rows : rows + META, 0 : 2 * rows].astype(F32)
        hot, gated = spread(meta, expert, rows)
        both = jnp.concatenate([hot.astype(BF), gated.astype(BF)], axis=0)
        got = dot(both, ref[i, 0:rows, :]).astype(BF)
        row = (jx * sources + jm) * CAP
        routed[row : row + CAP, :] = got[0:CAP]
        weighted_ref[0, row : row + CAP, :] = got[CAP:]
    depth = own_ref.shape[1]
    mine = pl.ds(pl.multiple_of(x * depth, 128), depth)
    theirs = pl.ds(pl.multiple_of((1 - x) * depth, 128), depth)
    own = own_ref[0, :, pl.ds(pl.multiple_of(x * half, 128), half)]
    back = dot(routed[:, mine], own) + dot(routed[:, theirs], other)
    size = sources * CAP
    part_ref[0, 0] = back[0:size].astype(part_ref.dtype)
    part_ref[1, 0] = back[size:].astype(part_ref.dtype)


def grad_kernel(rows_of, idx, *refs):
    keep_ref, send_ref, total = refs[-3:]
    refs = list(refs[:-3])
    z, x = idx[0], idx[1]
    nz = len(rows_of)
    outer = (z == 0) | (z == nz - 1)
    weighted = [refs.pop(0) for _ in range(nz)]
    acts = []
    for count in rows_of:
        act = refs.pop(0)[0]
        acts.append(jnp.where(outer, act, refs.pop(0)[0]) if count == 2 else act)
    step = min(256, total.shape[0])
    for n in range(0, total.shape[0], step):
        acc = sum(dot(act, w[0, :, n : n + step]) for act, w in zip(acts, weighted))
        total[n : n + step, :] = acc.T.astype(BF)
    depth = total.shape[0] // 2
    keep_ref[0] = total[pl.ds(pl.multiple_of(x * depth, 16), depth), :]
    send_ref[0] = total[pl.ds(pl.multiple_of((1 - x) * depth, 16), depth), :]


def join_kernel(half, idx, keep_ref, got_ref, out_ref):
    x = idx[1]
    out_ref[0, :, pl.ds(pl.multiple_of(x * half, 128), half)] = keep_ref[0]
    out_ref[0, :, pl.ds(pl.multiple_of((1 - x) * half, 128), half)] = got_ref[0]


def last_kernel(rows, n_in, again, idx, gate_ref, up_ref, meta_ref, *refs):
    ins, (pre_ref, score_ref, late) = refs[:n_in], refs[-3:]
    count = gate_ref.shape[2]
    m = idx[2]

    @pl.when(pl.program_id(1) == 0)
    def _():
        r = lax.broadcasted_iota(jnp.int32, (CAP, 128), 0)
        c = lax.broadcasted_iota(jnp.int32, (CAP, 128), 1)
        for i in range(2):
            meta = meta_ref[i].astype(F32)
            at = i ^ (m % 2)
            span = slice(i * CAP, (i + 1) * CAP)
            for e in range(count):
                _, gated = spread(meta, m * count + e, rows)
                if again:
                    back = ins[0][e, span].astype(F32)
                else:
                    back = sum(o[0, e, span].astype(F32) for o in ins)
                g = gate_ref[0, at, e].astype(F32)
                u = up_ref[0, at, e].astype(F32)
                sig = lax.logistic(g)
                silu = g * sig
                score = jnp.sum(back * (silu * u), axis=1, keepdims=True)
                grad = jnp.sum(gated, axis=1, keepdims=True) * back
                pre_ref[0, at, e] = (grad * u * sig * (1.0 + g * (1.0 - sig))).astype(BF)
                late[at, e] = (grad * silu).astype(BF)
                line = jnp.sum(jnp.where(r == c, score, 0.0), axis=0, keepdims=True)
                score_ref[i, e : e + 1, :] = line + ins[1][i, e : e + 1, :] if again else line

    @pl.when(pl.program_id(1) == 1)
    def _():
        pre_ref[0] = late[...]


def gate_kernel(rows, idx, ids_ref, *refs):
    out_ref = refs[-1]
    m = idx[2]
    cols = named(ids_ref[...], rows)
    r = lax.broadcasted_iota(jnp.int32, (rows, rows), 0)
    c = lax.broadcasted_iota(jnp.int32, (rows, rows), 1)
    before = dot((c < r).astype(BF), sum(cols).astype(BF))
    lanes = lax.broadcasted_iota(jnp.int32, (rows, 128), 1).astype(F32)
    at = lax.broadcasted_iota(jnp.int32, (rows, EXPERTS), 1)
    slots = [jnp.sum(col * before, axis=1, keepdims=True) for col in cols]
    names = [jnp.sum(jnp.where(col > 0.5, at, 0), axis=1, keepdims=True) for col in cols]
    outs = [jnp.zeros((rows, 1), F32) for _ in cols]
    for jm, ref in enumerate(refs[:-1]):
        for e in range(ref.shape[0]):
            expert = (m ^ jm) * ref.shape[0] + e
            line = ref[e : e + 1, :]
            for k in range(len(cols)):
                hit = (lanes == slots[k]) & (names[k] == expert)
                outs[k] = outs[k] + jnp.sum(jnp.where(hit, line, 0.0), axis=1, keepdims=True)
    for k, o in enumerate(outs):
        out_ref[:, k : k + 1] = o


def call(name, kernel, grid, in_specs, out_specs, out_shape, scratch=(), mib=20, alias=None, flops=0, moved=0):
    return pl.pallas_call(
        kernel,
        name=name,
        grid_spec=pltpu.PrefetchScalarGridSpec(
            num_scalar_prefetch=1,
            grid=grid,
            in_specs=in_specs,
            out_specs=out_specs,
            scratch_shapes=list(scratch),
        ),
        out_shape=out_shape,
        compiler_params=params(mib),
        input_output_aliases=alias or {},
        cost_estimate=pl.CostEstimate(flops=flops, bytes_accessed=moved, transcendentals=0),
    )


def after(v, *deps):
    return lax.optimization_barrier((v, *deps))[0]


def whole(shape):
    return pl.BlockSpec(shape, lambda *_: (0,) * len(shape))


def shards(out_grad, expert_ids, gate_weights, saved_acts, down_weight):
    sources = lax.axis_size("expert")
    n_dp = lax.axis_size("dp")
    nz = n_dp // 2
    line = nz == 4
    count, depth, width = down_weight.shape
    half = width // 2
    rows, model = out_grad.shape
    part = model // nz
    top = expert_ids.shape[1]
    size = sources * CAP
    lots, per = 1, count
    cuts = 2 if count % 2 == 0 else 1
    cut = count // cuts
    dp, m = lax.axis_index("dp"), lax.axis_index("expert")
    z, x = dp // 2, dp % 2
    idx = jnp.stack([z, x, m]).astype(jnp.int32)

    def move_z(v, pairs, name):
        with jax.named_scope(name):
            return lax.ppermute(v, "dp", [(2 * a + i, 2 * b + i) for a, b in pairs for i in range(2)])

    def flip_z(v, k, name):
        return move_z(v, [(a, a ^ k) for a in range(nz)], name)

    def flip_x(v, name):
        with jax.named_scope(name):
            return lax.ppermute(v, "dp", [(i, i ^ 1) for i in range(n_dp)])

    def flip_m(v, k, name):
        with jax.named_scope(name):
            return lax.ppermute(v, "expert", [(i, i ^ k) for i in range(sources)])

    inner = [(1, 2), (2, 1)]
    inward = [(0, 1), (3, 2)]
    outward = [(1, 0), (2, 3)]

    act_shape = jax.ShapeDtypeStruct((count, size, half), BF)
    act_spec = pl.BlockSpec((count, CAP, half), lambda j, idx: (0, j, 0))
    saved_spec = pl.BlockSpec((1, 1, count, CAP, 2 * width), lambda j, idx: (0, idx[2] ^ j, 0, 0, 0))
    keep, send = call(
        "act",
        functools.partial(act_kernel, half),
        (sources,),
        [saved_spec],
        [act_spec, act_spec],
        [act_shape, act_shape],
    )(idx, saved_acts)

    pieces = call(
        "pack",
        functools.partial(pack_kernel, rows, part),
        (1,),
        [whole((rows, model)), whole((rows, top)), whole((rows, top))],
        [whole((rows + META, part))] * nz,
        [jax.ShapeDtypeStruct((rows + META, part), BF)] * nz,
    )(idx, out_grad, expert_ids, gate_weights)

    bits = []
    bit = sources // 2
    while bit:
        bits.append(bit)
        bit //= 2
    def order_of(steps):
        seen = [(0, 0)]
        for bit in steps:
            seen = seen + [(jx ^ (bit == 0), jm ^ bit) for jx, jm in seen]
        return seen

    steps = {k: [0, *bits] if k else [bits[0], 0, *bits[1:]] for k in range(nz)}
    places = {k: order_of(steps[k]) for k in range(nz)}
    nb = 2 * sources
    parts, weighted = {}, {}
    near, far = {}, {}

    def route(k):
        blocks = pl.BlockSpec((nb // 2, rows + META, part), lambda e, idx: (0, 0, 0))
        quarter = pl.BlockSpec((nb // 4, rows + META, part), lambda e, idx: (0, 0, 0))
        wire = k and (k == nz - 1 or not line)
        out = call(
            f"route{k}",
            functools.partial(route_kernel, rows, places[k], count, half, cut),
            (count,),
            [blocks, quarter, quarter, pl.BlockSpec((1, depth, width), lambda e, idx: (e, 0, 0))]
            + [
                pl.BlockSpec((1, depth, half), lambda e, idx, i=i: (jnp.clip(e - i * cut, 0, cut - 1), 0, 0))
                for i in range(cuts)
            ],
            [
                pl.BlockSpec((2, 1, size, half), lambda e, idx: (0, e, 0, 0)),
                pl.BlockSpec((1, 2 * size, part), lambda e, idx: (e, 0, 0)),
            ],
            [
                jax.ShapeDtypeStruct((2, count, size, half), BF if wire else F32),
                jax.ShapeDtypeStruct((count, 2 * size, part), BF),
            ],
            [pltpu.VMEM((2 * size, part), BF)],
            mib=20 if line else 48,
        )(idx, near[k], *far[k], down_weight, *other_w)
        weighted[k] = out[1]
        return out[0]

    weights = [
        lax.dynamic_slice(down_weight, (h * cut, 0, (1 - x) * half), (cut, depth, half))
        for h in range(cuts)
    ]
    first = nz - 1
    come = {0: pieces[0], first: flip_z(pieces[first], first, f"rows{first}_z")}
    act_got = flip_x(send, "act_x")
    other_w = [flip_x(weights[0], "weight0_x")]
    flat_spec = pl.BlockSpec((1, size, half), lambda e: (e, 0, 0))
    pair_spec = pl.BlockSpec((1, half, 2 * size), lambda e: (e, 0, 0))
    own_act = pl.pallas_call(
        pair_kernel,
        name="pair",
        grid=(count,),
        in_specs=[flat_spec, flat_spec],
        out_specs=pair_spec,
        out_shape=jax.ShapeDtypeStruct((count, half, 2 * size), BF),
        compiler_params=params(16),
    )(keep, act_got)
    if line:
        r1 = flip_z(own_act, 1, "act_z_r1")
        i3 = move_z(after(own_act, come[3]), inner, "act_z_i3")
        come[1] = flip_z(after(pieces[1], r1), 1, "rows1_z")
    else:
        for k in range(first - 1, 0, -1):
            come[k] = flip_z(after(pieces[k], come[first]), k, f"rows{k}_z")
        acts = [[own_act]] + [[flip_z(own_act, k, f"act_z{k}")] for k in range(1, nz)]

    def plus(v, got):
        return (v.astype(F32) + got.astype(F32)).astype(BF)

    ties = {}

    chains = {"x": [], "y": []}

    def stage(k, at):
        bit = steps[k][at]
        link = "x" if bit == 0 else "y" if bit == bits[0] else "c"
        tied = [*chains.get(link, []), *ties.get((link, k), [])]
        if at == 0:
            v = after(come[k][None], *tied)
        else:
            v = jnp.concatenate([near[k], *(after(u, *tied) for u in far[k])], axis=0)
        sent = [v]
        if at == len(steps[k]) - 1:
            sent = [v[: v.shape[0] // 2], v[v.shape[0] // 2 :]]
        if bit == 0:
            far[k] = [flip_x(u, f"rows{k}_x") for u in sent]
        else:
            far[k] = [flip_m(u, bit, f"rows{k}_expert{bit}") for u in sent]
        near[k] = v
        if link in chains:
            chains[link] = [far[k][-1]]

    def rest(k, start):
        for at in range(start, len(steps[k])):
            stage(k, at)

    if line:
        stage(0, 0)
    stage(first, 0)
    come3_x = far[first][0]
    if line:
        come[2] = flip_z(after(pieces[2], come3_x), 2, "rows2_z")
        ties["y", 3] = [other_w[0]]
        ties["c", 3] = [r1, i3]
    if cuts > 1:
        other_w.append(flip_x(after(weights[1], other_w[0], come3_x), "weight1_x"))
        chains["x"] = [other_w[-1]]
    rest(first, 1)
    parts[first, 0] = route(first)
    if line:
        s1 = [move_z(parts[3, 0], inward, "back_s1")]
        ties["x", 2] = [parts[3, 0]]
        stage(2, 0)
        o2 = move_z(i3, outward, "act_z_o2")
        i2 = move_z(r1, inner, "act_z_i2")
        stage(1, 0)
        stage(0, 1)
        come1_x, come0_x = far[1][0], far[0][0]
        stage(2, 1)
        ties["c", 2] = [come1_x, come0_x, *s1]
        rest(2, 2)
        parts[2, 0] = route(2)
        v2 = [plus(parts[2, 0], s1[0])]
        s2_in = [move_z(v2[0], inward, "back_s2_in")]
        s2_mid = [move_z(v2[0], inner, "back_s2_mid")]
        stage(1, 1)
        o3 = move_z(after(i2, *s1), outward, "act_z_o3")
        ties["c", 1] = [parts[2, 0], o2, i2]
        rest(1, 2)
        acts = [[own_act], [r1], [o2, i2], [o3, i3]]
        parts[1, 0] = route(1)
        ties["c", 0] = [*far[1]]
        rest(0, 2)
        near[0] = after(near[0], o3)
        parts[0, 0] = route(0)
    else:
        for k in range(first - 1, -1, -1):
            rest(k, 0)
            parts[k, 0] = route(k)

    flat = [weighted[k] for k in range(nz)]
    specs = [pl.BlockSpec((1, 2 * size, part), lambda e, idx: (e, 0, 0))] * nz
    for act in acts:
        flat += act
        specs += [pl.BlockSpec((1, half, 2 * size), lambda e, idx: (e, 0, 0))] * len(act)
    g_spec = pl.BlockSpec((1, depth, half), lambda e, idx: (e, 0, 0))
    g_shape = jax.ShapeDtypeStruct((count, depth, half), BF)
    g_keep, g_send = call(
        "down_grad",
        functools.partial(grad_kernel, [len(a) for a in acts]),
        (count,),
        specs,
        [g_spec, g_spec],
        [g_shape, g_shape],
        [pltpu.VMEM((part, half), BF)],
        mib=22 if line else 60,
        flops=2 * count * nz * 2 * size * part * half,
        moved=sum(v.size * 2 for v in flat),
    )(idx, *flat)
    if line:
        v3 = [plus(parts[1, h], s2_mid[h]) for h in range(lots)]
        v4 = [plus(parts[3, h], s2_in[h]) for h in range(lots)]
        v3[0] = after(v3[0], g_send)
        v4[0] = after(v4[0], g_send)
        got = [
            [flip_z(v3[h], 1, f"back{h}_s3_flip"), move_z(v4[h], inner, f"back{h}_s3_mid")]
            for h in range(lots)
        ]
    else:
        got = [[flip_z(parts[k, h], k, f"back{h}_{k}") for k in range(1, nz)] for h in range(lots)]
    owns = [[parts[0, h]] + got[h] for h in range(lots)]

    g_got = flip_x(g_send, "grad_x")
    down_grad = call(
        "join",
        functools.partial(join_kernel, half),
        (count,),
        [g_spec, g_spec],
        pl.BlockSpec((1, depth, width), lambda e, idx: (e, 0, 0)),
        jax.ShapeDtypeStruct((count, depth, width), BF),
    )(idx, g_keep, g_got)

    outgoing = [sum(o[1].astype(F32) for o in own).astype(BF) for own in owns]
    outgoing[0] = after(outgoing[0], g_got)
    other = [flip_x(outgoing[h], f"back{h}_x") for h in range(lots)]

    order = {jm: at for at, (jx, jm) in enumerate(places[0]) if jx == 0}
    blocks = [(v, i) for v in (near[0], *far[0]) for i in range(v.shape[0])]

    def meta_of(jm):
        ref, i = blocks[order[jm]]
        return ref[i, rows:, 0 : 2 * rows]

    meta = jnp.stack([meta_of(jm) for jm in range(sources)])
    score_spec = pl.BlockSpec((2, count, 128), lambda j, p, idx: (j, 0, 0))

    def owner(ins, in_specs, again, before):
        def side(idx):
            return 1 - idx[1] if again else idx[1]

        def lanes(up):
            return pl.BlockSpec(
                (1, 2, count, CAP, half), lambda j, p, idx: (0, (idx[2] // 2) ^ j, 0, 0, side(idx) + 2 * up)
            )

        return call(
            "owner_other" if again else "owner_own",
            functools.partial(last_kernel, rows, len(ins), again),
            (sources // 2, 2),
            [lanes(0), lanes(1), pl.BlockSpec((2, META, 2 * rows), lambda j, p, idx: (j, 0, 0))]
            + in_specs
            + [pl.BlockSpec(memory_space=pl.ANY)] * len(before),
            [
                pl.BlockSpec(
                    (1, 2, count, CAP, half), lambda j, p, idx: (0, (idx[2] // 2) ^ j, 0, 0, side(idx) + 2 * p)
                ),
                score_spec,
            ],
            [
                jax.ShapeDtypeStruct(saved_acts.shape, BF),
                jax.ShapeDtypeStruct((sources, count, 128), F32),
            ],
            [pltpu.VMEM((2, count, CAP, half), BF)],
            alias={4 + len(ins): 0} if again else {},
        )(idx, saved_acts, saved_acts, meta, *ins, *before)

    own_spec = pl.BlockSpec((1, count, 2 * CAP, half), lambda j, p, idx: (0, 0, j, 0))
    early, partial_scores = owner(owns[0], [own_spec] * len(owns[0]), False, [])
    other_spec = pl.BlockSpec((count, 2 * CAP, half), lambda j, p, idx: (0, j, 0))
    late = after(other[0], down_grad, partial_scores)
    pre_grads, scores = owner([late, partial_scores], [other_spec, score_spec], True, [early])
    returned = [scores[0]] + [flip_m(scores[j], j, f"score{j}") for j in range(1, sources)]
    gate_grad = call(
        "gate_grad",
        functools.partial(gate_kernel, rows),
        (1,),
        [whole((rows, top))] + [whole((count, 128))] * sources,
        whole((rows, top)),
        jax.ShapeDtypeStruct((rows, top), F32),
    )(idx, expert_ids, *returned)
    return (pre_grads, down_grad, gate_grad)


def solution(mesh):
    placed = (
        P(("dp", "expert"), None),
        P(("dp", "expert"), None),
        P(("dp", "expert"), None),
        P("dp", None, "expert", None, None),
        P("expert", "dp", None),
    )
    return jax.shard_map(
        shards,
        mesh=mesh,
        in_specs=placed,
        out_specs=(
            P("dp", None, "expert", None, None),
            P("expert", "dp", None),
            P(("dp", "expert"), None),
        ),
        check_vma=False,
    )
```
